32 devices in a mesh: groups: 2 (over y), space: 4 (over z), dp: 2 (over x), chan: 2 (over core).
Axes of the slice: x: 2, y: 2, z: 4, core: 2. Of those that a mesh axis runs over, the one named last changes fastest.
Arguments:
- coarse: bfloat16 [4, 4, 4, 8, 512], P(('groups', 'dp'), 'space'), parts along dimension 0, may hold values from -6 to 6
- skip: bfloat16 [4, 8, 16, 8, 256], P(('groups', 'dp'), 'space', None, None, 'chan'), parts along dimension 0, may hold values from -6 to 6
- up_weight: bfloat16 [8, 512, 2, 128], P(None, 'space', 'chan', 'dp'), may hold values from -0.25 to 0.25
- up_bias: float32 [256], P('chan'), may hold values from -3 to 3
- first_weight: bfloat16 [27, 512, 2, 128], P(None, 'space', 'chan', 'dp'), may hold values from -0.0546875 to 0.0546875
- first_bias: float32 [256], P('chan'), may hold values from -3 to 3
- second_weight: bfloat16 [27, 256, 2, 128], P(None, 'space', 'chan', 'dp'), may hold values from -0.078125 to 0.078125
- second_bias: float32 [256], P('chan'), may hold values from -3 to 3
Outputs:
- refined: bfloat16 [4, 8, 16, 8, 256], P(('groups', 'dp'), 'space', None, None, 'chan'), parts along dimension 0
The draws below stay inside these ranges and needn't reach their ends.
There are 2 independent parts, one for each index of `groups`. The reference program is written for one: setup_inputs(seed, part) draws one part's arguments, and reference() takes and returns one part's arrays. A program takes and returns all parts, laid end to end along the dimension named above; an argument that names none is the same for every part. Nothing has to cross between parts.
All inputs are finite; a program needn't handle non-finite values.
Results may differ from the reference program's by a relative error of at most 0.0045.
Values may be sent and summed in bfloat16 or wider, within the bound.
No kernel may reach another device: no remote copies, remote signals or barrier semaphores. Data moves between devices by JAX's collectives and lax.ppermute only.
A program may use at most 64 MiB of HBM per device.

```python
import jax
import jax.numpy as jnp
from jax import lax

CIN = 512
COUT = 256
CY = 8
SUBVOLS = 2
CX = 4
CZ = 4
FX = 8
FY = 16
FZ = 8
HALF = 128
N_CHAN = 2


def steps_of(rng, extent, split, low, largest):
    gain, own = 1.0, jax.random.fold_in(rng, 6)
    for dim, shards_of in split:
        heights = jnp.exp(jax.random.uniform(jax.random.fold_in(own, dim), (shards_of,), jnp.float32, low / len(split), largest / len(split)))
        gain = gain * jnp.repeat(heights, extent[dim] // shards_of).reshape([-1 if axis == dim else 1 for axis in range(len(extent))])
    return gain


def normal_values(stream_key, extent, deviation, bound, cuts=(), held_as=jnp.bfloat16):
    result = deviation * jax.random.normal(stream_key, extent, jnp.float32)
    if cuts:
        result = result * steps_of(stream_key, extent, cuts, -0.22, 0.18)
    return jnp.clip(result, -bound, bound).astype(held_as)


def setup_inputs(seed: int = 0, part: int = 0) -> dict:
    arg_keys = jax.random.split(jax.random.key(seed), 9)
    own_keys = jax.random.split(jax.random.fold_in(arg_keys[8], part), 9)
    return {
        "coarse": normal_values(own_keys[0], (SUBVOLS, CZ, CX, CY, CIN), 1.0, 6.0, ((0, 2), (1, 4))),
        "skip": normal_values(own_keys[1], (SUBVOLS, FX, FY, FZ, COUT), 1.0, 6.0, ((0, 2), (1, 4), (4, 2))),
        "up_weight": normal_values(arg_keys[2], (8, CIN, N_CHAN, HALF), CIN ** -0.5, 0.25, ((1, 4), (2, 2), (3, 2))),
        "up_bias": normal_values(arg_keys[3], (COUT,), 0.5, 3.0, ((0, 2),), jnp.float32),
        "first_weight": normal_values(arg_keys[4], (27, 2 * COUT, N_CHAN, HALF), (54 * COUT) ** -0.5, 0.0546875, ((1, 4), (2, 2), (3, 2))),
        "first_bias": normal_values(arg_keys[5], (COUT,), 0.5, 3.0, ((0, 2),), jnp.float32),
        "second_weight": normal_values(arg_keys[6], (27, COUT, N_CHAN, HALF), (27 * COUT) ** -0.5, 0.078125, ((1, 4), (2, 2), (3, 2))),
        "second_bias": normal_values(arg_keys[7], (COUT,), 0.5, 3.0, ((0, 2),), jnp.float32),
    }


def alternate(total, bias):
    samples, depth_cells, width_cells, height_cells, taps, outputs = total.shape
    grid = total.reshape(samples, depth_cells, width_cells, height_cells, 2, 2, 2, outputs)
    grid = grid.transpose(0, 2, 4, 3, 5, 1, 6, 7)
    grid = grid.reshape(samples, 2 * width_cells, 2 * height_cells, 2 * depth_cells, outputs)
    return (grid + bias).astype(jnp.bfloat16)


def convolve(features, weight, inputs):
    kernel = weight.reshape(3, 3, 3, inputs, COUT).astype(jnp.float32)
    return lax.conv_general_dilated(features.astype(jnp.float32), kernel, (1, 1, 1), [(1, 1), (1, 1), (1, 1)], dimension_numbers=("NDHWC", "DHWIO", "NDHWC"), precision=lax.Precision.HIGHEST)


def reference(coarse, skip, up_weight, up_bias, first_weight, first_bias, second_weight, second_bias):
    up_matrix = up_weight.reshape(8, CIN, COUT).astype(jnp.float32)
    total = jnp.einsum("szxyi,kio->szxyko", coarse.astype(jnp.float32), up_matrix, precision=lax.Precision.HIGHEST)
    upsampled = alternate(total, up_bias)
    joined = jnp.concatenate([upsampled, skip], axis=4)
    hidden = jax.nn.silu(convolve(joined, first_weight, 2 * COUT) + first_bias).astype(jnp.bfloat16)
    return (convolve(hidden, second_weight, COUT) + second_bias).astype(jnp.bfloat16)
```

```python
import jax
import jax.numpy as jnp
from jax import lax
from jax.sharding import PartitionSpec as P


def padded_2(array, sides, width):
    for axis, dim in sides:
        peers, length = (lax.axis_size(axis), array.shape[dim])
        up = [(i, (i + 1) % peers) for i in range(peers - 1)]
        down = [(j, i) for i, j in up]
        last = lax.slice_in_dim(array, length - width, length, axis=dim)
        first = lax.slice_in_dim(array, 0, width, axis=dim)
        before = lax.ppermute(last, axis, up)
        after = lax.ppermute(first, axis, down)
        array = jnp.concatenate([before, array, after], axis=dim)
    return array


def alternate(total, bias):
    samples, depth_cells, width_cells, height_cells, taps, outputs = total.shape
    grid = total.reshape(samples, depth_cells, width_cells, height_cells, 2, 2, 2, outputs)
    grid = grid.transpose(0, 2, 4, 3, 5, 1, 6, 7)
    grid = grid.reshape(samples, 2 * width_cells, 2 * height_cells, 2 * depth_cells, outputs)
    return (grid + bias).astype(jnp.bfloat16)


def upsample_block(coarse, up_weight):
    columns = lax.all_gather(up_weight, "dp", axis=3, tiled=True)[:, :, 0, :]
    initial = jnp.zeros(coarse.shape[:4] + (8, columns.shape[2]), jnp.float32)

    def accumulate(summed, weight_rows, offset):
        return jnp.einsum(
            "szxyi,kio->szxyko", coarse, weight_rows, preferred_element_type=jnp.float32
        )

    return accumulate(initial, lax.all_gather(columns, "space", axis=1, tiled=True), jnp.int32(0))


def spatial_conv(padded, weight_block):
    kernel = weight_block.reshape(3, 3, 3, weight_block.shape[1], weight_block.shape[2])
    return lax.conv_general_dilated(
        padded,
        kernel,
        (1, 1, 1),
        [(0, 0), (1, 1), (1, 1)],
        dimension_numbers=("NDHWC", "DHWIO", "NDHWC"),
        preferred_element_type=jnp.float32,
    )


def folded_conv(padded, columns, base_shape):
    initial = jnp.zeros(base_shape + (columns.shape[2],), jnp.float32)

    def accumulate(summed, weight_rows, offset):
        sliced = lax.dynamic_slice_in_dim(padded, offset, weight_rows.shape[1], 4)
        return summed + spatial_conv(sliced, weight_rows)

    return (accumulate, initial)


def body(coarse, skip, up_weight, up_bias, first_weight, first_bias, second_weight, second_bias):
    slabs = lax.all_to_all(coarse, "space", split_axis=2, concat_axis=1, tiled=True)
    upsampled = alternate(upsample_block(slabs, up_weight), up_bias)
    up_full, skip_full = (
        lax.all_gather(upsampled, "chan", axis=4, tiled=True),
        lax.all_gather(skip, "chan", axis=4, tiled=True),
    )
    joined = jnp.concatenate([up_full, skip_full], axis=4)
    padded = padded_2(joined, (("space", 1),), 1)
    base_shape = joined.shape[:4]
    first_columns = lax.all_gather(first_weight, "dp", axis=3, tiled=True)[:, :, 0, :]
    accumulate, initial = folded_conv(padded, first_columns, base_shape)
    first = accumulate(
        initial, lax.all_gather(first_columns, "space", axis=1, tiled=True), jnp.int32(0)
    )
    hidden = jax.nn.silu(first + first_bias).astype(jnp.bfloat16)
    hidden_full = lax.all_gather(hidden, "chan", axis=4, tiled=True)
    hidden_padded = padded_2(hidden_full, (("space", 1),), 1)
    second_columns = lax.all_gather(second_weight, "dp", axis=3, tiled=True)[:, :, 0, :]
    accumulate_two, initial_two = folded_conv(hidden_padded, second_columns, base_shape)
    second = accumulate_two(
        initial_two, lax.all_gather(second_columns, "space", axis=1, tiled=True), jnp.int32(0)
    )
    return (second + second_bias).astype(jnp.bfloat16)


def swapped(array, axis):
    return lax.ppermute(array, axis, [(0, 1), (1, 0)])


def ordered(index, own, other, axis=0):
    first = jnp.where(index == 0, own, other)
    second = jnp.where(index == 0, other, own)
    return jnp.stack([first, second], axis=axis)


def line_routes():
    early, late = ([], [])
    for s in range(4):
        for d in range(2):
            for c in range(2):
                source = (s * 2 + d) * 2 + c
                up_target = (c * 2 + d) * 2 + s % 2
                skip_target = ((2 + c) * 2 + d) * 2 + s % 2
                early.append((source, up_target if s < 2 else skip_target))
                late.append((source, skip_target if s < 2 else up_target))
    return early, late


def conv_block(features, weight):
    return lax.conv_general_dilated(
        features[None],
        weight,
        (1, 1, 1),
        [(1, 1), (1, 1), (1, 1)],
        dimension_numbers=("NDHWC", "DHWOI", "NDHWC"),
        preferred_element_type=jnp.float32,
    )[0]


def stationary(
    coarse, skip, up_weight, up_bias, first_weight, first_bias, second_weight, second_bias
):
    s, d, c = (lax.axis_index(a) for a in ("space", "dp", "chan"))
    group = ("space", "dp", "chan")
    _, _, cx, cy, cin = coarse.shape
    cz = 4
    _, bx, fy, fz, half = skip.shape
    fx = 4 * bx
    cells = cx * cy
    block = bx * fy * fz
    taps = up_weight.shape[0]
    kb = up_weight.shape[1]
    own_n = up_weight.shape[3]
    lanes = 128
    up_rows = taps * own_n
    first_own = first_weight[:, :, 0, :].transpose(0, 2, 1)
    second_own = second_weight[:, :, 0, :]
    first_other = swapped(first_own, "dp")
    up_rows_own = up_weight[:, :, 0, :].transpose(0, 2, 1).reshape(up_rows, kb)
    coarse_rows = coarse.reshape(cells, cin // kb, kb).transpose(1, 0, 2).reshape(-1, kb)
    up_packet = jnp.concatenate([up_rows_own, coarse_rows], axis=0)
    skip_rows = skip.reshape(block, half)
    skip_packet = jnp.pad(skip_rows, ((0, up_packet.shape[0] - block), (0, 0)))
    early_route, late_route = line_routes()
    early = lax.ppermute(jnp.where(s < 2, up_packet, skip_packet), group, early_route)
    late = lax.ppermute(jnp.where(s < 2, skip_packet, up_packet), group, late_route)
    weights = []
    for packet in (early, late):
        own = packet[:up_rows]
        other = swapped(own, "dp")
        both = ordered(d, own.reshape(taps, own_n, kb), other.reshape(taps, own_n, kb), 1)
        weights.append(both.reshape(taps, 2 * own_n, kb))
    weights = jnp.stack(weights)
    second_other = swapped(second_own, "dp")
    slabs = jnp.stack([early[up_rows:], late[up_rows:]]).reshape(2, 2, 2, cells, kb)
    mine = lax.dynamic_index_in_dim(slabs, c, 2, keepdims=False)
    theirs = lax.dynamic_index_in_dim(slabs, 1 - c, 2, keepdims=False)
    slabs = ordered(c, mine, swapped(theirs, "chan"), 1)
    up = jnp.einsum("zwkmi,ktoi->zwmto", slabs, weights, preferred_element_type=jnp.float32)
    up = up + jnp.where(c == s, up_bias, 0.0)
    up = up.reshape(cz, cx, cy, 2, 2, 2, half).transpose(1, 3, 2, 4, 0, 5, 6)
    up = up.reshape(fx * fy * fz, half)
    blocks = jnp.stack([late[:block], early[:block]])
    nothing = jnp.zeros_like(blocks)
    placed = ordered(c, blocks, nothing, 1).reshape(fx * fy * fz, half)
    part = jnp.where(s < 2, up, placed.astype(jnp.float32))
    joined = (part + swapped(part, "chan")).astype(jnp.bfloat16)
    joined = joined.reshape(fx, fy, fz, half)
    first_kernel = jnp.concatenate([first_own, first_other], axis=1)
    first = conv_block(joined, first_kernel.reshape(3, 3, 3, half, half))
    bias = first_bias.reshape(2, own_n)
    bias = jnp.where(d == 0, bias.reshape(-1), bias[::-1].reshape(-1))
    first = (first + jnp.where(s == 0, bias, 0.0)).astype(jnp.bfloat16)
    first = first.reshape(2, 2, block, 2, own_n).transpose(0, 3, 2, 1, 4)
    first = first.reshape(2, 2, block, half)
    mine = lax.dynamic_index_in_dim(first, c, 0, keepdims=False)
    theirs = lax.dynamic_index_in_dim(first, 1 - c, 0, keepdims=False)
    chunks = ordered(c, mine, swapped(theirs, "chan"), 0)
    chunks = ordered(d, chunks[:, 0], chunks[:, 1], 1).reshape(4, block, half)
    terms = lax.all_to_all(chunks, "space", split_axis=0, concat_axis=0, tiled=True)
    hidden = jax.nn.silu(jnp.sum(terms.astype(jnp.float32), axis=0)).astype(jnp.bfloat16)
    hidden = ordered(c, hidden, swapped(hidden, "chan"), 0)
    hidden = hidden.reshape(2, block, 2, own_n).transpose(0, 2, 1, 3)
    hidden = hidden.reshape(fx, fy, fz, own_n)
    second_kernel = jnp.concatenate([second_own, second_other], axis=2).transpose(0, 2, 1)
    second = conv_block(hidden, second_kernel.reshape(3, 3, 3, half, own_n))
    second = second.astype(jnp.bfloat16).reshape(4, block, half)
    terms = lax.all_to_all(second, "space", split_axis=0, concat_axis=0, tiled=True)
    total = jnp.sum(terms.astype(jnp.float32), axis=0)
    total = jnp.where(d == 0, total, jnp.roll(total, own_n, axis=1))
    return (total + second_bias).astype(jnp.bfloat16).reshape(skip.shape)


def keeps_weights(mesh):
    sizes = tuple(mesh.shape[a] for a in ("space", "dp", "chan"))
    return sizes == (4, 2, 2)


def solution(mesh):
    return jax.shard_map(
        stationary if keeps_weights(mesh) else body,
        mesh=mesh,
        in_specs=(
            P(("groups", "dp"), "space", None, None, None),
            P(("groups", "dp"), "space", None, None, "chan"),
            P(None, "space", "chan", "dp"),
            P("chan"),
            P(None, "space", "chan", "dp"),
            P("chan"),
            P(None, "space", "chan", "dp"),
            P("chan"),
        ),
        out_specs=P(("groups", "dp"), "space", None, None, "chan"),
        check_vma=False,
    )
```

```python
import jax
import jax.numpy as jnp
from jax import lax
from jax.experimental import pallas as pl
from jax.experimental.pallas import tpu as pltpu
from jax.sharding import PartitionSpec as P


def padded_2(array, sides, width):
    for axis, dim in sides:
        peers, length = (lax.axis_size(axis), array.shape[dim])
        up = [(i, (i + 1) % peers) for i in range(peers - 1)]
        down = [(j, i) for i, j in up]
        last = lax.slice_in_dim(array, length - width, length, axis=dim)
        first = lax.slice_in_dim(array, 0, width, axis=dim)
        before = lax.ppermute(last, axis, up)
        after = lax.ppermute(first, axis, down)
        array = jnp.concatenate([before, array, after], axis=dim)
    return array


def alternate(total, bias):
    samples, depth_cells, width_cells, height_cells, taps, outputs = total.shape
    grid = total.reshape(samples, depth_cells, width_cells, height_cells, 2, 2, 2, outputs)
    grid = grid.transpose(0, 2, 4, 3, 5, 1, 6, 7)
    grid = grid.reshape(samples, 2 * width_cells, 2 * height_cells, 2 * depth_cells, outputs)
    return (grid + bias).astype(jnp.bfloat16)


def upsample_block(coarse, up_weight):
    columns = lax.all_gather(up_weight, "dp", axis=3, tiled=True)[:, :, 0, :]
    initial = jnp.zeros(coarse.shape[:4] + (8, columns.shape[2]), jnp.float32)

    def accumulate(summed, weight_rows, offset):
        return jnp.einsum(
            "szxyi,kio->szxyko", coarse, weight_rows, preferred_element_type=jnp.float32
        )

    return accumulate(initial, lax.all_gather(columns, "space", axis=1, tiled=True), jnp.int32(0))


def spatial_conv(padded, weight_block):
    kernel = weight_block.reshape(3, 3, 3, weight_block.shape[1], weight_block.shape[2])
    return lax.conv_general_dilated(
        padded,
        kernel,
        (1, 1, 1),
        [(0, 0), (1, 1), (1, 1)],
        dimension_numbers=("NDHWC", "DHWIO", "NDHWC"),
        preferred_element_type=jnp.float32,
    )


def folded_conv(padded, columns, base_shape):
    initial = jnp.zeros(base_shape + (columns.shape[2],), jnp.float32)

    def accumulate(summed, weight_rows, offset):
        sliced = lax.dynamic_slice_in_dim(padded, offset, weight_rows.shape[1], 4)
        return summed + spatial_conv(sliced, weight_rows)

    return (accumulate, initial)


def body(coarse, skip, up_weight, up_bias, first_weight, first_bias, second_weight, second_bias):
    slabs = lax.all_to_all(coarse, "space", split_axis=2, concat_axis=1, tiled=True)
    upsampled = alternate(upsample_block(slabs, up_weight), up_bias)
    up_full, skip_full = (
        lax.all_gather(upsampled, "chan", axis=4, tiled=True),
        lax.all_gather(skip, "chan", axis=4, tiled=True),
    )
    joined = jnp.concatenate([up_full, skip_full], axis=4)
    padded = padded_2(joined, (("space", 1),), 1)
    base_shape = joined.shape[:4]
    first_columns = lax.all_gather(first_weight, "dp", axis=3, tiled=True)[:, :, 0, :]
    accumulate, initial = folded_conv(padded, first_columns, base_shape)
    first = accumulate(
        initial, lax.all_gather(first_columns, "space", axis=1, tiled=True), jnp.int32(0)
    )
    hidden = jax.nn.silu(first + first_bias).astype(jnp.bfloat16)
    hidden_full = lax.all_gather(hidden, "chan", axis=4, tiled=True)
    hidden_padded = padded_2(hidden_full, (("space", 1),), 1)
    second_columns = lax.all_gather(second_weight, "dp", axis=3, tiled=True)[:, :, 0, :]
    accumulate_two, initial_two = folded_conv(hidden_padded, second_columns, base_shape)
    second = accumulate_two(
        initial_two, lax.all_gather(second_columns, "space", axis=1, tiled=True), jnp.int32(0)
    )
    return (second + second_bias).astype(jnp.bfloat16)


def swapped(array, axis):
    return lax.ppermute(array, axis, [(0, 1), (1, 0)])


def ordered(index, own, other, axis=0):
    first = jnp.where(index == 0, own, other)
    second = jnp.where(index == 0, other, own)
    return jnp.stack([first, second], axis=axis)


def line_routes():
    early, late = ([], [])
    for s in range(4):
        for d in range(2):
            for c in range(2):
                source = (s * 2 + d) * 2 + c
                up_target = (c * 2 + d) * 2 + s % 2
                skip_target = ((2 + c) * 2 + d) * 2 + s % 2
                early.append((source, up_target if s < 2 else skip_target))
                late.append((source, skip_target if s < 2 else up_target))
    return early, late


NT = (((1,), (1,)), ((), ()))
NN = (((1,), (0,)), ((), ()))


def first_kernel(mine, theirs, own, other, bias, out, even, odd):
    planes = even.shape[0] - 2
    rows, width = even.shape[1:]
    half = mine.shape[1]
    quad = planes // 4
    blank = jnp.zeros((1,) + odd.shape[1:], odd.dtype)
    odd[0:1] = blank
    odd[planes + 1 : planes + 2] = blank
    even[0:1] = blank[:, :rows]
    even[planes + 1 : planes + 2] = blank[:, :rows]
    cell = lax.broadcasted_iota(jnp.int32, (rows, half), 0) % 8
    edge = jnp.zeros((8, width), jnp.float32)
    for x in range(planes):
        plane = mine[x * rows : (x + 1) * rows] + theirs[x * rows : (x + 1) * rows]
        plane = plane.astype(jnp.bfloat16).astype(jnp.float32)
        below = jnp.where(cell == 0, 0.0, pltpu.roll(plane, 1, 0))
        above = jnp.where(cell == 7, 0.0, pltpu.roll(plane, rows - 1, 0))
        taps = jnp.concatenate([below, plane, above], axis=1)
        even[x + 1] = taps.astype(jnp.bfloat16)
        odd[x + 1] = jnp.concatenate([edge, taps, edge], axis=0).astype(jnp.bfloat16)
    lane = lax.broadcasted_iota(jnp.int32, (2 * quad * rows, half), 1)
    for q in range(2):
        total = jnp.broadcast_to(bias[...], (4 * quad * rows // 2, half))
        total = None
        for dx in range(3):
            for dy in range(3):
                at = pl.ds(q * 2 * quad + dx, 2 * quad)
                if dy == 1:
                    left = even[at]
                else:
                    left = odd[at, pl.ds(8 * dy, rows)]
                left = left.reshape(2 * quad * rows, width)
                tap = (dx * 3 + dy) * 3
                right = jnp.concatenate(
                    [jnp.concatenate([own[tap + dz], other[tap + dz]], axis=0) for dz in range(3)],
                    axis=1,
                )
                term = lax.dot_general(left, right, NT, preferred_element_type=jnp.float32)
                total = term if total is None else total + term
        total = total + bias[...]
        low, high = (total[: quad * rows], total[quad * rows :])
        lane = lax.broadcasted_iota(jnp.int32, low.shape, 1)
        swap = half // 2
        out[q, 0] = jnp.where(lane < swap, low, pltpu.roll(high, swap, 1)).astype(jnp.bfloat16)
        out[q, 1] = jnp.where(lane < swap, pltpu.roll(low, swap, 1), high).astype(jnp.bfloat16)


def first_conv(mine, theirs, own, other, bias, planes, fz):
    cells, half = mine.shape
    rows = cells // planes
    return pl.pallas_call(
        first_kernel,
        out_shape=jax.ShapeDtypeStruct((2, 2, cells // 4, half), jnp.bfloat16),
        in_specs=[pl.BlockSpec(memory_space=pltpu.VMEM)] * 5,
        out_specs=pl.BlockSpec(memory_space=pltpu.VMEM),
        scratch_shapes=[
            pltpu.VMEM((planes + 2, rows, 3 * half), jnp.bfloat16),
            pltpu.VMEM((planes + 2, rows + 16, 3 * half), jnp.bfloat16),
        ],
        compiler_params=pltpu.CompilerParams(vmem_limit_bytes=32 * 2**20),
    )(mine, theirs, own, other, bias)


def second_kernel(hidden, own, other, out, even, odd):
    planes = even.shape[0] - 2
    rows, width = even.shape[1:]
    lanes = hidden.shape[2]
    k = lanes // 2
    swap = lanes // 2
    d = lax.axis_index("dp")
    blank = jnp.zeros((1,) + odd.shape[1:], odd.dtype)
    odd[0:1] = blank
    odd[planes + 1 : planes + 2] = blank
    even[0:1] = blank[:, :rows]
    even[planes + 1 : planes + 2] = blank[:, :rows]
    cell = lax.broadcasted_iota(jnp.int32, (rows, lanes), 0) % 8
    lane = lax.broadcasted_iota(jnp.int32, (rows, lanes), 1)
    low = lane < swap
    edge = jnp.zeros((8, width), jnp.float32)
    per = hidden.shape[1] // rows
    for q in range(2):
        for r in range(per):
            packed = hidden[q, r * rows : (r + 1) * rows].astype(jnp.float32)
            turned = pltpu.roll(packed, swap, 1)
            for u in range(2):
                here, there = (packed, turned) if u == 0 else (turned, packed)
                below = jnp.where(cell == 0, 0.0, pltpu.roll(here, 1, 0))
                above = jnp.where(cell == 7, 0.0, pltpu.roll(here, rows - 1, 0))
                taps = jnp.concatenate(
                    [jnp.where(low, below, there), jnp.where(low, above, 0.0)], axis=1
                )
                x = (q * 2 + u) * per + r
                even[x + 1] = taps.astype(jnp.bfloat16)
                odd[x + 1] = jnp.concatenate([edge, taps, edge], axis=0).astype(jnp.bfloat16)
    lane_w = lax.broadcasted_iota(jnp.int32, (3 * k, lanes), 1)
    for q in range(2):
        total = None
        for dx in range(3):
            for dy in range(3):
                at = pl.ds(q * planes // 2 + dx, planes // 2)
                if dy == 1:
                    left = even[at]
                else:
                    left = odd[at, pl.ds(8 * dy, rows)]
                left = left.reshape(planes // 2 * rows, width)[:, : 3 * k]
                tap = (dx * 3 + dy) * 3
                one = own[tap : tap + 3].reshape(3 * k, k)
                two = other[tap : tap + 3].reshape(3 * k, k)
                right = jnp.concatenate(
                    [jnp.where(d == 0, one, two), jnp.where(d == 0, two, one)], axis=1
                )
                term = lax.dot_general(left, right, NN, preferred_element_type=jnp.float32)
                total = term if total is None else total + term
        n = planes // 2 * rows
        out[q * n : (q + 1) * n] = total.astype(jnp.bfloat16)


def second_conv(hidden, own, other, planes):
    _, rows2, lanes = hidden.shape
    cells = rows2 * 4
    rows = cells // planes
    return pl.pallas_call(
        second_kernel,
        out_shape=jax.ShapeDtypeStruct((cells, lanes), jnp.bfloat16),
        in_specs=[pl.BlockSpec(memory_space=pltpu.VMEM)] * 3,
        out_specs=pl.BlockSpec(memory_space=pltpu.VMEM),
        scratch_shapes=[
            pltpu.VMEM((planes + 2, rows, 2 * lanes), jnp.bfloat16),
            pltpu.VMEM((planes + 2, rows + 16, 2 * lanes), jnp.bfloat16),
        ],
        compiler_params=pltpu.CompilerParams(vmem_limit_bytes=32 * 2**20),
    )(hidden, own, other)


def stationary(
    coarse, skip, up_weight, up_bias, first_weight, first_bias, second_weight, second_bias
):
    s, d, c = (lax.axis_index(a) for a in ("space", "dp", "chan"))
    group = ("space", "dp", "chan")
    _, _, cx, cy, cin = coarse.shape
    cz = 4
    _, bx, fy, fz, half = skip.shape
    fx = 4 * bx
    cells = cx * cy
    block = bx * fy * fz
    taps = up_weight.shape[0]
    kb = up_weight.shape[1]
    own_n = up_weight.shape[3]
    lanes = 128
    up_rows = taps * own_n
    first_own = first_weight[:, :, 0, :].transpose(0, 2, 1)
    second_own = second_weight[:, :, 0, :]
    first_other = swapped(first_own, "dp")
    up_rows_own = up_weight[:, :, 0, :].transpose(0, 2, 1).reshape(up_rows, kb)
    coarse_rows = coarse.reshape(cells, cin // kb, kb).transpose(1, 0, 2).reshape(-1, kb)
    up_packet = jnp.concatenate([up_rows_own, coarse_rows], axis=0)
    skip_rows = skip.reshape(block, half)
    skip_packet = jnp.pad(skip_rows, ((0, up_packet.shape[0] - block), (0, 0)))
    early_route, late_route = line_routes()
    early = lax.ppermute(jnp.where(s < 2, up_packet, skip_packet), group, early_route)
    late = lax.ppermute(jnp.where(s < 2, skip_packet, up_packet), group, late_route)
    weights = []
    for packet in (early, late):
        own = packet[:up_rows]
        other = swapped(own, "dp")
        both = ordered(d, own.reshape(taps, own_n, kb), other.reshape(taps, own_n, kb), 1)
        weights.append(both.reshape(taps, 2 * own_n, kb))
    weights = jnp.stack(weights)
    second_other = swapped(second_own, "dp")
    slabs = jnp.stack([early[up_rows:], late[up_rows:]]).reshape(2, 2, 2, cells, kb)
    mine = lax.dynamic_index_in_dim(slabs, c, 2, keepdims=False)
    theirs = lax.dynamic_index_in_dim(slabs, 1 - c, 2, keepdims=False)
    slabs = ordered(c, mine, swapped(theirs, "chan"), 1)
    up = jnp.einsum("zwkmi,ktoi->zwmto", slabs, weights, preferred_element_type=jnp.float32)
    up = up + jnp.where(c == s, up_bias, 0.0)
    up = up.reshape(cz, cx, cy, 2, 2, 2, half).transpose(1, 3, 2, 4, 0, 5, 6)
    up = up.reshape(fx * fy * fz, half)
    blocks = jnp.stack([late[:block], early[:block]])
    nothing = jnp.zeros_like(blocks)
    placed = ordered(c, blocks, nothing, 1).reshape(fx * fy * fz, half)
    part = jnp.where(s < 2, up, placed.astype(jnp.float32))
    bias = first_bias.reshape(2, own_n)
    bias = jnp.where(d == 0, bias.reshape(-1), bias[::-1].reshape(-1))
    bias = jnp.where(s == 0, bias, 0.0)[None]
    first = first_conv(part, swapped(part, "chan"), first_own, first_other, bias, fx, fz)
    mine = lax.dynamic_index_in_dim(first, c, 0, keepdims=False)
    theirs = lax.dynamic_index_in_dim(first, 1 - c, 0, keepdims=False)
    chunks = ordered(c, mine, swapped(theirs, "chan"), 0)
    chunks = ordered(d, chunks[:, 0], chunks[:, 1], 1).reshape(4, block, half)
    terms = lax.all_to_all(chunks, "space", split_axis=0, concat_axis=0, tiled=True)
    hidden = jax.nn.silu(jnp.sum(terms.astype(jnp.float32), axis=0)).astype(jnp.bfloat16)
    hidden = ordered(c, hidden, swapped(hidden, "chan"), 0)
    second = second_conv(hidden, second_own, second_other, fx)
    second = second.reshape(4, block, half)
    terms = lax.all_to_all(second, "space", split_axis=0, concat_axis=0, tiled=True)
    total = jnp.sum(terms.astype(jnp.float32), axis=0)
    return (total + second_bias).astype(jnp.bfloat16).reshape(skip.shape)


def keeps_weights(mesh):
    sizes = tuple(mesh.shape[a] for a in ("space", "dp", "chan"))
    return sizes == (4, 2, 2)


def solution(mesh):
    return jax.shard_map(
        stationary if keeps_weights(mesh) else body,
        mesh=mesh,
        in_specs=(
            P(("groups", "dp"), "space", None, None, None),
            P(("groups", "dp"), "space", None, None, "chan"),
            P(None, "space", "chan", "dp"),
            P("chan"),
            P(None, "space", "chan", "dp"),
            P("chan"),
            P(None, "space", "chan", "dp"),
            P("chan"),
        ),
        out_specs=P(("groups", "dp"), "space", None, None, "chan"),
        check_vma=False,
    )
```

```python
import jax
import jax.numpy as jnp
from jax import lax
from jax.experimental import pallas as pl
from jax.experimental.pallas import tpu as pltpu
from jax.sharding import PartitionSpec as P


def padded_2(array, sides, width):
    for axis, dim in sides:
        peers, length = (lax.axis_size(axis), array.shape[dim])
        up = [(i, (i + 1) % peers) for i in range(peers - 1)]
        down = [(j, i) for i, j in up]
        last = lax.slice_in_dim(array, length - width, length, axis=dim)
        first = lax.slice_in_dim(array, 0, width, axis=dim)
        before = lax.ppermute(last, axis, up)
        after = lax.ppermute(first, axis, down)
        array = jnp.concatenate([before, array, after], axis=dim)
    return array


def alternate(total, bias):
    samples, depth_cells, width_cells, height_cells, taps, outputs = total.shape
    grid = total.reshape(samples, depth_cells, width_cells, height_cells, 2, 2, 2, outputs)
    grid = grid.transpose(0, 2, 4, 3, 5, 1, 6, 7)
    grid = grid.reshape(samples, 2 * width_cells, 2 * height_cells, 2 * depth_cells, outputs)
    return (grid + bias).astype(jnp.bfloat16)


def upsample_block(coarse, up_weight):
    columns = lax.all_gather(up_weight, "dp", axis=3, tiled=True)[:, :, 0, :]
    initial = jnp.zeros(coarse.shape[:4] + (8, columns.shape[2]), jnp.float32)

    def accumulate(summed, weight_rows, offset):
        return jnp.einsum(
            "szxyi,kio->szxyko", coarse, weight_rows, preferred_element_type=jnp.float32
        )

    return accumulate(initial, lax.all_gather(columns, "space", axis=1, tiled=True), jnp.int32(0))


def spatial_conv(padded, weight_block):
    kernel = weight_block.reshape(3, 3, 3, weight_block.shape[1], weight_block.shape[2])
    return lax.conv_general_dilated(
        padded,
        kernel,
        (1, 1, 1),
        [(0, 0), (1, 1), (1, 1)],
        dimension_numbers=("NDHWC", "DHWIO", "NDHWC"),
        preferred_element_type=jnp.float32,
    )


def folded_conv(padded, columns, base_shape):
    initial = jnp.zeros(base_shape + (columns.shape[2],), jnp.float32)

    def accumulate(summed, weight_rows, offset):
        sliced = lax.dynamic_slice_in_dim(padded, offset, weight_rows.shape[1], 4)
        return summed + spatial_conv(sliced, weight_rows)

    return (accumulate, initial)


def body(coarse, skip, up_weight, up_bias, first_weight, first_bias, second_weight, second_bias):
    slabs = lax.all_to_all(coarse, "space", split_axis=2, concat_axis=1, tiled=True)
    upsampled = alternate(upsample_block(slabs, up_weight), up_bias)
    up_full, skip_full = (
        lax.all_gather(upsampled, "chan", axis=4, tiled=True),
        lax.all_gather(skip, "chan", axis=4, tiled=True),
    )
    joined = jnp.concatenate([up_full, skip_full], axis=4)
    padded = padded_2(joined, (("space", 1),), 1)
    base_shape = joined.shape[:4]
    first_columns = lax.all_gather(first_weight, "dp", axis=3, tiled=True)[:, :, 0, :]
    accumulate, initial = folded_conv(padded, first_columns, base_shape)
    first = accumulate(
        initial, lax.all_gather(first_columns, "space", axis=1, tiled=True), jnp.int32(0)
    )
    hidden = jax.nn.silu(first + first_bias).astype(jnp.bfloat16)
    hidden_full = lax.all_gather(hidden, "chan", axis=4, tiled=True)
    hidden_padded = padded_2(hidden_full, (("space", 1),), 1)
    second_columns = lax.all_gather(second_weight, "dp", axis=3, tiled=True)[:, :, 0, :]
    accumulate_two, initial_two = folded_conv(hidden_padded, second_columns, base_shape)
    second = accumulate_two(
        initial_two, lax.all_gather(second_columns, "space", axis=1, tiled=True), jnp.int32(0)
    )
    return (second + second_bias).astype(jnp.bfloat16)


def swapped(array, axis):
    return lax.ppermute(array, axis, [(0, 1), (1, 0)])


def ordered(index, own, other, axis=0):
    first = jnp.where(index == 0, own, other)
    second = jnp.where(index == 0, other, own)
    return jnp.stack([first, second], axis=axis)


def pack_kernel(weight, coarse, skip, first, biases, early, late, half, held, sems):
    s = lax.axis_index("space")
    g = lax.axis_index("groups")
    kb = early.shape[1]
    rows, deep = (weight.shape[0], coarse.shape[0])
    span = half.shape[0]

    def fill(up_packet, skip_packet):
        moves = [(weight, up_packet.at[pl.ds(0, rows)])]
        for i in range(coarse.shape[1] // kb):
            place = up_packet.at[pl.ds(rows + i * deep, deep)]
            moves.append((coarse.at[:, pl.ds(i * kb, kb)], place))
        moves.append((skip, skip_packet.at[pl.ds(0, skip.shape[0])]))
        rest = skip_packet.shape[0] - skip.shape[0]
        moves.append((weight.at[pl.ds(0, rest)], skip_packet.at[pl.ds(skip.shape[0], rest)]))
        moves.append((first.at[pl.ds(g * (first.shape[0] - span), span)], half))
        for i, bias in enumerate(biases):
            moves.append((bias, held.at[pl.ds(i, 1)]))
        copies = [
            pltpu.make_async_copy(source, place, sems.at[i])
            for i, (source, place) in enumerate(moves)
        ]
        for copy in copies:
            copy.start()
        for copy in copies:
            copy.wait()

    @pl.when(s < 2)
    def _():
        fill(early, late)

    @pl.when(s >= 2)
    def _():
        fill(late, early)


def packed(weight, coarse, skip, first, biases):
    rows, kb = weight.shape
    deep, cin = coarse.shape
    count = len(biases)
    packet = jax.ShapeDtypeStruct((rows + deep * (cin // kb), kb), jnp.bfloat16)
    span = (first.shape[0] + 1) // 2
    half = jax.ShapeDtypeStruct((span,) + first.shape[1:], jnp.bfloat16)
    held = jax.ShapeDtypeStruct((count,) + biases[0].shape[1:], jnp.float32)

    def kernel(*refs):
        pack_kernel(*refs[:4], refs[4 : 4 + count], *refs[4 + count :])

    return pl.pallas_call(
        kernel,
        out_shape=(packet, packet, half, held),
        in_specs=[pl.BlockSpec(memory_space=pltpu.HBM)] * (4 + count),
        out_specs=[pl.BlockSpec(memory_space=pltpu.VMEM)] * 4,
        scratch_shapes=[pltpu.SemaphoreType.DMA((4 + cin // kb + count,))],
        compiler_params=pltpu.CompilerParams(vmem_limit_bytes=60 * 2**20),
    )(weight, coarse, skip, first, *biases)


def dense_kernel(weight, out):
    deep = weight.shape[1] // 2
    for tap in range(weight.shape[0]):
        out[tap] = jnp.concatenate([weight[tap, :deep], weight[tap, deep:]], axis=1)


def dense(weight):
    taps, rows, lanes = weight.shape
    return pl.pallas_call(
        dense_kernel,
        out_shape=jax.ShapeDtypeStruct((taps, rows // 2, 2 * lanes), weight.dtype),
        in_specs=[pl.BlockSpec(memory_space=pltpu.VMEM)],
        out_specs=pl.BlockSpec(memory_space=pltpu.VMEM),
        compiler_params=pltpu.CompilerParams(vmem_limit_bytes=16 * 2**20),
    )(weight)


def up_kernel(early, late, early_other, late_other, slabs, held, part):
    s, d, c = (lax.axis_index(a) for a in ("space", "dp", "chan"))
    rows, kb = early_other.shape
    deep = slabs.shape[2]
    taps = 8
    own_n = rows // taps
    half = part.shape[1]
    block = part.shape[0] // 4

    @pl.when(s < 2)
    def _():
        lefts, rights = ([], [])
        for k in range(2):
            pieces = []
            for parity in range(2):
                for i, packet in enumerate((early, late)):
                    low = packet[pl.ds(rows + 2 * k * deep, deep)]
                    high = packet[pl.ds(rows + (2 * k + 1) * deep, deep)]
                    mine = jnp.where(c == 0, low, high)
                    pieces.append(jnp.where(c == parity, mine, slabs[i, k]))
            lefts.append(jnp.concatenate(pieces, axis=0))
            packet, other = ((early, early_other), (late, late_other))[k]
            pieces = []
            for tap in range(taps):
                one = packet[pl.ds(tap * own_n, own_n)]
                two = other[pl.ds(tap * own_n, own_n)]
                pieces += [jnp.where(d == 0, one, two), jnp.where(d == 0, two, one)]
            rights.append(jnp.concatenate(pieces, axis=0))
        left = jnp.concatenate(lefts, axis=1)
        right = jnp.concatenate(rights, axis=1)
        bias = held[0:1] * jnp.where(c == s, 1.0, 0.0)
        for tap in range(taps):
            a, b, cc = (tap // 4, tap // 2 % 2, tap % 2)
            total = lax.dot_general(
                left,
                right[tap * 2 * own_n : (tap + 1) * 2 * own_n],
                NT,
                preferred_element_type=jnp.float32,
            )
            total = total + bias
            for parity in range(2):
                for i in range(2):
                    z = 2 * (parity + 2 * i) + cc
                    for x in range(deep // 8):
                        at = (parity * 2 + i) * deep + x * 8
                        start = ((2 * x + a) * 16 + b) * 8 + z
                        part[pl.ds(start, 8, 16)] = total[at : at + 8]

    @pl.when(s >= 2)
    def _():
        for i, packet in enumerate((late, early)):
            values = packet[pl.ds(0, block)].astype(jnp.float32)
            for parity in range(2):
                place = pl.ds((2 * i + parity) * block, block)
                part[place] = jnp.where(c == parity, values, 0.0)


def up_part(early, late, early_other, late_other, slabs, held, cells):
    return pl.pallas_call(
        up_kernel,
        out_shape=jax.ShapeDtypeStruct((cells, held.shape[1]), jnp.float32),
        in_specs=[pl.BlockSpec(memory_space=pltpu.VMEM)] * 6,
        out_specs=pl.BlockSpec(memory_space=pltpu.VMEM),
        compiler_params=pltpu.CompilerParams(vmem_limit_bytes=32 * 2**20),
    )(early, late, early_other, late_other, slabs, held)


def reduced(chunk_for, s):
    total = chunk_for(s).astype(jnp.float32)
    for step in (3, 2, 1):
        routes = [(i, i ^ step) for i in range(4)]
        term = lax.ppermute(chunk_for(s ^ step), "space", routes)
        total = total + term.astype(jnp.float32)
    return total


def line_routes():
    early, late = ([], [])
    for s in range(4):
        for d in range(2):
            for c in range(2):
                source = (s * 2 + d) * 2 + c
                up_target = (c * 2 + d) * 2 + s % 2
                skip_target = ((2 + c) * 2 + d) * 2 + s % 2
                early.append((source, up_target if s < 2 else skip_target))
                late.append((source, skip_target if s < 2 else up_target))
    return early, late


NT = (((1,), (1,)), ((), ()))
NN = (((1,), (0,)), ((), ()))


def first_kernel(mine, theirs, own, near, far, held, out, even, odd):
    planes = even.shape[0] - 2
    rows, width = even.shape[1:]
    half = mine.shape[1]
    quad = planes // 4
    blank = jnp.zeros((1,) + odd.shape[1:], odd.dtype)
    odd[0:1] = blank
    odd[planes + 1 : planes + 2] = blank
    even[0:1] = blank[:, :rows]
    even[planes + 1 : planes + 2] = blank[:, :rows]
    cell = lax.broadcasted_iota(jnp.int32, (rows, half), 0) % 8
    edge = jnp.zeros((8, width), jnp.float32)
    for x in range(planes):
        plane = mine[x * rows : (x + 1) * rows] + theirs[x * rows : (x + 1) * rows]
        plane = plane.astype(jnp.bfloat16).astype(jnp.float32)
        below = jnp.where(cell == 0, 0.0, pltpu.roll(plane, 1, 0))
        above = jnp.where(cell == 7, 0.0, pltpu.roll(plane, rows - 1, 0))
        taps = jnp.concatenate([below, plane, above], axis=1)
        even[x + 1] = taps.astype(jnp.bfloat16)
        odd[x + 1] = jnp.concatenate([edge, taps, edge], axis=0).astype(jnp.bfloat16)
    s, d, g = (lax.axis_index(a) for a in ("space", "dp", "groups"))
    swap = half // 2
    bias = jnp.broadcast_to(held[1:2], (8, half))
    bias = jnp.where(d == 0, bias, pltpu.roll(bias, swap, 1))[0:1]
    bias = bias * jnp.where(s == 0, 1.0, 0.0)
    span, taps = (near.shape[0], own.shape[0])
    other = []
    for tap in range(taps):
        if tap < span:
            lower, upper = (near[tap], far[tap])
        else:
            lower, upper = (far[tap - taps + span], near[tap - taps + span])
        if tap == span - 1:
            upper = near[0]
        other.append(jnp.where(g == 0, lower, upper))
    for q in range(2):
        total = None
        for dx in range(3):
            for dy in range(3):
                at = pl.ds(q * 2 * quad + dx, 2 * quad)
                if dy == 1:
                    left = even[at]
                else:
                    left = odd[at, pl.ds(8 * dy, rows)]
                left = left.reshape(2 * quad * rows, width)
                tap = (dx * 3 + dy) * 3
                right = jnp.concatenate(
                    [jnp.concatenate([own[tap + dz], other[tap + dz]], axis=0) for dz in range(3)],
                    axis=1,
                )
                term = lax.dot_general(left, right, NT, preferred_element_type=jnp.float32)
                total = term if total is None else total + term
        total = total + bias
        low, high = (total[: quad * rows], total[quad * rows :])
        lane = lax.broadcasted_iota(jnp.int32, low.shape, 1)
        out[q, 0] = jnp.where(lane < swap, low, pltpu.roll(high, swap, 1)).astype(jnp.bfloat16)
        out[q, 1] = jnp.where(lane < swap, pltpu.roll(low, swap, 1), high).astype(jnp.bfloat16)


def first_conv(mine, theirs, own, near, far, held, planes):
    cells, half = mine.shape
    rows = cells // planes
    return pl.pallas_call(
        first_kernel,
        out_shape=jax.ShapeDtypeStruct((2, 2, cells // 4, half), jnp.bfloat16),
        in_specs=[pl.BlockSpec(memory_space=pltpu.VMEM)] * 6,
        out_specs=pl.BlockSpec(memory_space=pltpu.VMEM),
        scratch_shapes=[
            pltpu.VMEM((planes + 2, rows, 3 * half), jnp.bfloat16),
            pltpu.VMEM((planes + 2, rows + 16, 3 * half), jnp.bfloat16),
        ],
        compiler_params=pltpu.CompilerParams(vmem_limit_bytes=32 * 2**20),
    )(mine, theirs, own, near, far, held)


def second_kernel(hidden, own, other, held, out, even, odd):
    planes = even.shape[0] - 2
    rows, width = even.shape[1:]
    lanes = hidden.shape[2]
    k = lanes // 2
    swap = lanes // 2
    d = lax.axis_index("dp")
    blank = jnp.zeros((1,) + odd.shape[1:], odd.dtype)
    odd[0:1] = blank
    odd[planes + 1 : planes + 2] = blank
    even[0:1] = blank[:, :rows]
    even[planes + 1 : planes + 2] = blank[:, :rows]
    cell = lax.broadcasted_iota(jnp.int32, (rows, lanes), 0) % 8
    lane = lax.broadcasted_iota(jnp.int32, (rows, lanes), 1)
    low = lane < swap
    edge = jnp.zeros((8, width), jnp.float32)
    per = hidden.shape[1] // rows
    for q in range(2):
        for r in range(per):
            packed = hidden[q, r * rows : (r + 1) * rows].astype(jnp.float32)
            turned = pltpu.roll(packed, swap, 1)
            for u in range(2):
                here, there = (packed, turned) if u == 0 else (turned, packed)
                below = jnp.where(cell == 0, 0.0, pltpu.roll(here, 1, 0))
                above = jnp.where(cell == 7, 0.0, pltpu.roll(here, rows - 1, 0))
                taps = jnp.concatenate(
                    [jnp.where(low, below, there), jnp.where(low, above, 0.0)], axis=1
                )
                x = (q * 2 + u) * per + r
                even[x + 1] = taps.astype(jnp.bfloat16)
                odd[x + 1] = jnp.concatenate([edge, taps, edge], axis=0).astype(jnp.bfloat16)
    lane = lax.broadcasted_iota(jnp.int32, own.shape[1:], 1)
    low = lane < swap
    rights = []
    for tap in range(0, own.shape[0], 3):
        rows_in = []
        for dz in range(3):
            one = jnp.where(d == 0, own[tap + dz], other[tap + dz])
            two = jnp.where(d == 0, other[tap + dz], own[tap + dz])
            rows_in.append(jnp.where(low, one, pltpu.roll(two, swap, 1)))
            rows_in.append(jnp.where(low, pltpu.roll(one, swap, 1), two))
        rights.append(jnp.concatenate(rows_in, axis=0))
    for q in range(2):
        total = None
        for dx in range(3):
            for dy in range(3):
                at = pl.ds(q * planes // 2 + dx, planes // 2)
                if dy == 1:
                    left = even[at]
                else:
                    left = odd[at, pl.ds(8 * dy, rows)]
                left = left.reshape(planes // 2 * rows, width)[:, : 3 * k]
                right = rights[dx * 3 + dy]
                term = lax.dot_general(left, right, NN, preferred_element_type=jnp.float32)
                total = term if total is None else total + term
        total = total + held[2:3] * jnp.where(lax.axis_index("space") == 0, 1.0, 0.0)
        n = planes // 2 * rows
        out[q * n : (q + 1) * n] = total.astype(jnp.bfloat16)


def second_conv(hidden, own, other, held, planes):
    _, rows2, lanes = hidden.shape
    cells = rows2 * 4
    rows = cells // planes
    return pl.pallas_call(
        second_kernel,
        out_shape=jax.ShapeDtypeStruct((cells, lanes), jnp.bfloat16),
        in_specs=[pl.BlockSpec(memory_space=pltpu.VMEM)] * 4,
        out_specs=pl.BlockSpec(memory_space=pltpu.VMEM),
        scratch_shapes=[
            pltpu.VMEM((planes + 2, rows, 2 * lanes), jnp.bfloat16),
            pltpu.VMEM((planes + 2, rows + 16, 2 * lanes), jnp.bfloat16),
        ],
        compiler_params=pltpu.CompilerParams(vmem_limit_bytes=32 * 2**20),
    )(hidden, own, other, held)


def stationary(
    coarse, skip, up_weight, up_bias, first_weight, first_bias, second_weight, second_bias
):
    s, d, c = (lax.axis_index(a) for a in ("space", "dp", "chan"))
    group = ("space", "dp", "chan")
    _, _, cx, cy, cin = coarse.shape
    _, bx, fy, fz, half = skip.shape
    fx = 4 * bx
    cells = cx * cy
    block = bx * fy * fz
    taps, kb, _, own_n = up_weight.shape
    up_rows = taps * own_n
    first_own = first_weight[:, :, 0, :].transpose(0, 2, 1)
    early, late, near, held = packed(
        up_weight[:, :, 0, :].transpose(0, 2, 1).reshape(up_rows, kb),
        coarse.reshape(cells, cin),
        skip.reshape(block, half),
        first_own,
        [bias.reshape(1, half) for bias in (up_bias, first_bias, second_bias)],
    )
    early_route, late_route = line_routes()
    late = lax.ppermute(late, group, late_route)
    early = lax.ppermute(early, group, early_route)
    near = swapped(near, "dp")
    early_other = swapped(early[:up_rows], "dp")
    far = swapped(near, "groups")
    late, early_other = lax.optimization_barrier((late, early_other))
    late_other = swapped(late[:up_rows], "dp")
    second_raw, early = lax.optimization_barrier((second_weight[:, :, 0, :], early))
    second_own = dense(second_raw)
    second_own, late_other = lax.optimization_barrier((second_own, late_other))
    second_other = swapped(second_own, "dp")
    slabs = jnp.stack([early[up_rows:], late[up_rows:]]).reshape(2, 2, 2, cells, kb)
    theirs = lax.dynamic_index_in_dim(slabs, 1 - c, 2, keepdims=False)
    slabs, far = lax.optimization_barrier((swapped(theirs, "chan"), far))
    part = up_part(early, late, early_other, late_other, slabs, held, fx * fy * fz)
    first = first_conv(part, swapped(part, "chan"), first_own, near, far, held, fx)
    mine = lax.dynamic_index_in_dim(first, c, 0, keepdims=False)
    theirs = lax.dynamic_index_in_dim(first, 1 - c, 0, keepdims=False)
    theirs, second_other = lax.optimization_barrier((swapped(theirs, "chan"), second_other))
    chunks = jnp.stack([mine, theirs]).reshape(4, block, half)

    def chunk_for(plane):
        place = 2 * ((plane // 2) ^ c) + ((plane % 2) ^ d)
        return lax.dynamic_index_in_dim(chunks, place, 0, keepdims=False)

    hidden = jax.nn.silu(reduced(chunk_for, s)).astype(jnp.bfloat16)
    hidden = ordered(c, hidden, swapped(hidden, "chan"), 0)
    second = second_conv(hidden, second_own, second_other, held, fx).reshape(4, block, half)
    total = reduced(lambda plane: lax.dynamic_index_in_dim(second, plane, 0, keepdims=False), s)
    return total.astype(jnp.bfloat16).reshape(skip.shape)


def keeps_weights(mesh):
    sizes = tuple(mesh.shape[a] for a in ("groups", "space", "dp", "chan"))
    return sizes == (2, 4, 2, 2)


def solution(mesh):
    return jax.shard_map(
        stationary if keeps_weights(mesh) else body,
        mesh=mesh,
        in_specs=(
            P(("groups", "dp"), "space", None, None, None),
            P(("groups", "dp"), "space", None, None, "chan"),
            P(None, "space", "chan", "dp"),
            P("chan"),
            P(None, "space", "chan", "dp"),
            P("chan"),
            P(None, "space", "chan", "dp"),
            P("chan"),
        ),
        out_specs=P(("groups", "dp"), "space", None, None, "chan"),
        check_vma=False,
    )
```

```python
import jax
import jax.numpy as jnp
from jax import lax
from jax.experimental import pallas as pl
from jax.experimental.pallas import tpu as pltpu
from jax.sharding import PartitionSpec as P


def padded_2(array, sides, width):
    for axis, dim in sides:
        peers, length = (lax.axis_size(axis), array.shape[dim])
        up = [(i, (i + 1) % peers) for i in range(peers - 1)]
        down = [(j, i) for i, j in up]
        last = lax.slice_in_dim(array, length - width, length, axis=dim)
        first = lax.slice_in_dim(array, 0, width, axis=dim)
        before = lax.ppermute(last, axis, up)
        after = lax.ppermute(first, axis, down)
        array = jnp.concatenate([before, array, after], axis=dim)
    return array


def alternate(total, bias):
    samples, depth_cells, width_cells, height_cells, taps, outputs = total.shape
    grid = total.reshape(samples, depth_cells, width_cells, height_cells, 2, 2, 2, outputs)
    grid = grid.transpose(0, 2, 4, 3, 5, 1, 6, 7)
    grid = grid.reshape(samples, 2 * width_cells, 2 * height_cells, 2 * depth_cells, outputs)
    return (grid + bias).astype(jnp.bfloat16)


def upsample_block(coarse, up_weight):
    columns = lax.all_gather(up_weight, "dp", axis=3, tiled=True)[:, :, 0, :]
    initial = jnp.zeros(coarse.shape[:4] + (8, columns.shape[2]), jnp.float32)

    def accumulate(summed, weight_rows, offset):
        return jnp.einsum(
            "szxyi,kio->szxyko", coarse, weight_rows, preferred_element_type=jnp.float32
        )

    return accumulate(initial, lax.all_gather(columns, "space", axis=1, tiled=True), jnp.int32(0))


def spatial_conv(padded, weight_block):
    kernel = weight_block.reshape(3, 3, 3, weight_block.shape[1], weight_block.shape[2])
    return lax.conv_general_dilated(
        padded,
        kernel,
        (1, 1, 1),
        [(0, 0), (1, 1), (1, 1)],
        dimension_numbers=("NDHWC", "DHWIO", "NDHWC"),
        preferred_element_type=jnp.float32,
    )


def folded_conv(padded, columns, base_shape):
    initial = jnp.zeros(base_shape + (columns.shape[2],), jnp.float32)

    def accumulate(summed, weight_rows, offset):
        sliced = lax.dynamic_slice_in_dim(padded, offset, weight_rows.shape[1], 4)
        return summed + spatial_conv(sliced, weight_rows)

    return (accumulate, initial)


def body(coarse, skip, up_weight, up_bias, first_weight, first_bias, second_weight, second_bias):
    slabs = lax.all_to_all(coarse, "space", split_axis=2, concat_axis=1, tiled=True)
    upsampled = alternate(upsample_block(slabs, up_weight), up_bias)
    up_full, skip_full = (
        lax.all_gather(upsampled, "chan", axis=4, tiled=True),
        lax.all_gather(skip, "chan", axis=4, tiled=True),
    )
    joined = jnp.concatenate([up_full, skip_full], axis=4)
    padded = padded_2(joined, (("space", 1),), 1)
    base_shape = joined.shape[:4]
    first_columns = lax.all_gather(first_weight, "dp", axis=3, tiled=True)[:, :, 0, :]
    accumulate, initial = folded_conv(padded, first_columns, base_shape)
    first = accumulate(
        initial, lax.all_gather(first_columns, "space", axis=1, tiled=True), jnp.int32(0)
    )
    hidden = jax.nn.silu(first + first_bias).astype(jnp.bfloat16)
    hidden_full = lax.all_gather(hidden, "chan", axis=4, tiled=True)
    hidden_padded = padded_2(hidden_full, (("space", 1),), 1)
    second_columns = lax.all_gather(second_weight, "dp", axis=3, tiled=True)[:, :, 0, :]
    accumulate_two, initial_two = folded_conv(hidden_padded, second_columns, base_shape)
    second = accumulate_two(
        initial_two, lax.all_gather(second_columns, "space", axis=1, tiled=True), jnp.int32(0)
    )
    return (second + second_bias).astype(jnp.bfloat16)


def swapped(array, axis):
    return lax.ppermute(array, axis, [(0, 1), (1, 0)])


def ordered(index, own, other, axis=0):
    first = jnp.where(index == 0, own, other)
    second = jnp.where(index == 0, other, own)
    return jnp.stack([first, second], axis=axis)


def pack_kernel(weight, coarse, skip, first, biases, early, late, half, held, sems):
    s = lax.axis_index("space")
    g = lax.axis_index("groups")
    kb = early.shape[1]
    rows, deep = (weight.shape[0], coarse.shape[0])
    span = half.shape[0]

    def fill(up_packet, skip_packet):
        moves = [(weight, up_packet.at[pl.ds(0, rows)])]
        for i in range(coarse.shape[1] // kb):
            place = up_packet.at[pl.ds(rows + i * deep, deep)]
            moves.append((coarse.at[:, pl.ds(i * kb, kb)], place))
        moves.append((skip, skip_packet.at[pl.ds(0, skip.shape[0])]))
        rest = skip_packet.shape[0] - skip.shape[0]
        moves.append((weight.at[pl.ds(0, rest)], skip_packet.at[pl.ds(skip.shape[0], rest)]))
        moves.append((first.at[pl.ds(g * (first.shape[0] - span), span)], half))
        for i, bias in enumerate(biases):
            moves.append((bias, held.at[pl.ds(i, 1)]))
        copies = [
            pltpu.make_async_copy(source, place, sems.at[i])
            for i, (source, place) in enumerate(moves)
        ]
        for copy in copies:
            copy.start()
        for copy in copies:
            copy.wait()

    @pl.when(s < 2)
    def _():
        fill(early, late)

    @pl.when(s >= 2)
    def _():
        fill(late, early)


def packed(weight, coarse, skip, first, biases):
    rows, kb = weight.shape
    deep, cin = coarse.shape
    count = len(biases)
    packet = jax.ShapeDtypeStruct((rows + deep * (cin // kb), kb), jnp.bfloat16)
    span = (first.shape[0] + 1) // 2
    half = jax.ShapeDtypeStruct((span,) + first.shape[1:], jnp.bfloat16)
    held = jax.ShapeDtypeStruct((count,) + biases[0].shape[1:], jnp.float32)

    def kernel(*refs):
        pack_kernel(*refs[:4], refs[4 : 4 + count], *refs[4 + count :])

    return pl.pallas_call(
        kernel,
        out_shape=(packet, packet, half, held),
        in_specs=[pl.BlockSpec(memory_space=pltpu.HBM)] * (4 + count),
        out_specs=[pl.BlockSpec(memory_space=pltpu.VMEM)] * 4,
        scratch_shapes=[pltpu.SemaphoreType.DMA((4 + cin // kb + count,))],
        compiler_params=pltpu.CompilerParams(vmem_limit_bytes=60 * 2**20),
    )(weight, coarse, skip, first, *biases)


def dense_kernel(weight, out):
    deep = weight.shape[1] // 2
    for tap in range(weight.shape[0]):
        out[tap] = jnp.concatenate([weight[tap, :deep], weight[tap, deep:]], axis=1)


def dense(weight):
    taps, rows, lanes = weight.shape
    return pl.pallas_call(
        dense_kernel,
        out_shape=jax.ShapeDtypeStruct((taps, rows // 2, 2 * lanes), weight.dtype),
        in_specs=[pl.BlockSpec(memory_space=pltpu.VMEM)],
        out_specs=pl.BlockSpec(memory_space=pltpu.VMEM),
        compiler_params=pltpu.CompilerParams(vmem_limit_bytes=16 * 2**20),
    )(weight)


def up_kernel(early, late, early_other, late_other, slabs, held, part):
    s, d, c = (lax.axis_index(a) for a in ("space", "dp", "chan"))
    rows, kb = early_other.shape
    deep = slabs.shape[1] // 4
    taps = 8
    own_n = rows // taps
    half = part.shape[1]
    block = part.shape[0] // 4

    @pl.when(s < 2)
    def _():
        lefts, rights = ([], [])
        for k in range(2):
            pieces = []
            for parity in range(2):
                for i, packet in enumerate((early, late)):
                    low = packet[pl.ds(rows + 2 * k * deep, deep)]
                    high = packet[pl.ds(rows + (2 * k + 1) * deep, deep)]
                    mine = jnp.where(c == 0, low, high)
                    low = slabs[i, pl.ds(2 * k * deep, deep)]
                    high = slabs[i, pl.ds((2 * k + 1) * deep, deep)]
                    theirs = jnp.where(c == 0, low, high)
                    pieces.append(jnp.where(c == parity, mine, theirs))
            lefts.append(jnp.concatenate(pieces, axis=0))
            packet, other = ((early, early_other), (late, late_other))[k]
            pieces = []
            for tap in range(taps):
                one = packet[pl.ds(tap * own_n, own_n)]
                two = other[pl.ds(tap * own_n, own_n)]
                pieces += [jnp.where(d == 0, one, two), jnp.where(d == 0, two, one)]
            rights.append(jnp.concatenate(pieces, axis=0))
        left = jnp.concatenate(lefts, axis=1)
        right = jnp.concatenate(rights, axis=1)
        bias = held[0:1] * jnp.where(c == s, 1.0, 0.0)
        for tap in range(taps):
            a, b, cc = (tap // 4, tap // 2 % 2, tap % 2)
            total = lax.dot_general(
                left,
                right[tap * 2 * own_n : (tap + 1) * 2 * own_n],
                NT,
                preferred_element_type=jnp.float32,
            )
            total = total + bias
            for parity in range(2):
                for i in range(2):
                    z = 2 * (parity + 2 * i) + cc
                    for x in range(deep // 8):
                        at = (parity * 2 + i) * deep + x * 8
                        start = ((2 * x + a) * 16 + b) * 8 + z
                        part[pl.ds(start, 8, 16)] = total[at : at + 8]

    @pl.when(s >= 2)
    def _():
        for i, packet in enumerate((late, early)):
            values = packet[pl.ds(0, block)].astype(jnp.float32)
            for parity in range(2):
                place = pl.ds((2 * i + parity) * block, block)
                part[place] = jnp.where(c == parity, values, 0.0)


def up_part(early, late, early_other, late_other, slabs, held, cells):
    return pl.pallas_call(
        up_kernel,
        out_shape=jax.ShapeDtypeStruct((cells, held.shape[1]), jnp.float32),
        in_specs=[pl.BlockSpec(memory_space=pltpu.VMEM)] * 6,
        out_specs=pl.BlockSpec(memory_space=pltpu.VMEM),
        compiler_params=pltpu.CompilerParams(vmem_limit_bytes=32 * 2**20),
    )(early, late, early_other, late_other, slabs, held)


def reduced(chunk_for, s):
    total = chunk_for(s).astype(jnp.float32)
    for step in (3, 2, 1):
        routes = [(i, i ^ step) for i in range(4)]
        term = lax.ppermute(chunk_for(s ^ step), "space", routes)
        total = total + term.astype(jnp.float32)
    return total


def line_routes():
    early, late, cross = ([], [], [])
    for s in range(4):
        for d in range(2):
            for c in range(2):
                source = (s * 2 + d) * 2 + c
                up_target = (c * 2 + d) * 2 + s % 2
                skip_target = ((2 + c) * 2 + d) * 2 + s % 2
                early.append((source, up_target if s < 2 else skip_target))
                late.append((source, skip_target if s < 2 else up_target))
                if s < 2:
                    cross.append((source, (c * 2 + 1 - d) * 2 + s % 2))
    return early, late, cross


NT = (((1,), (1,)), ((), ()))
NN = (((1,), (0,)), ((), ()))


def first_kernel(mine, theirs, own, near, far, held, out, even, odd):
    planes = even.shape[0] - 2
    rows, width = even.shape[1:]
    half = mine.shape[1]
    quad = planes // 4
    blank = jnp.zeros((1,) + odd.shape[1:], odd.dtype)
    odd[0:1] = blank
    odd[planes + 1 : planes + 2] = blank
    even[0:1] = blank[:, :rows]
    even[planes + 1 : planes + 2] = blank[:, :rows]
    cell = lax.broadcasted_iota(jnp.int32, (rows, half), 0) % 8
    edge = jnp.zeros((8, width), jnp.float32)
    for x in range(planes):
        plane = mine[x * rows : (x + 1) * rows] + theirs[x * rows : (x + 1) * rows]
        plane = plane.astype(jnp.bfloat16).astype(jnp.float32)
        below = jnp.where(cell == 0, 0.0, pltpu.roll(plane, 1, 0))
        above = jnp.where(cell == 7, 0.0, pltpu.roll(plane, rows - 1, 0))
        taps = jnp.concatenate([below, plane, above], axis=1)
        even[x + 1] = taps.astype(jnp.bfloat16)
        odd[x + 1] = jnp.concatenate([edge, taps, edge], axis=0).astype(jnp.bfloat16)
    s, d, g = (lax.axis_index(a) for a in ("space", "dp", "groups"))
    swap = half // 2
    bias = jnp.broadcast_to(held[1:2], (8, half))
    bias = jnp.where(d == 0, bias, pltpu.roll(bias, swap, 1))[0:1]
    bias = bias * jnp.where(s == 0, 1.0, 0.0)
    span, taps = (near.shape[0], own.shape[0])
    other = []
    for tap in range(taps):
        if tap < span:
            lower, upper = (near[tap], far[tap])
        else:
            lower, upper = (far[tap - taps + span], near[tap - taps + span])
        if tap == span - 1:
            upper = near[0]
        other.append(jnp.where(g == 0, lower, upper))
    for q in range(2):
        total = None
        for dx in range(3):
            for dy in range(3):
                at = pl.ds(q * 2 * quad + dx, 2 * quad)
                if dy == 1:
                    left = even[at]
                else:
                    left = odd[at, pl.ds(8 * dy, rows)]
                left = left.reshape(2 * quad * rows, width)
                tap = (dx * 3 + dy) * 3
                right = jnp.concatenate(
                    [jnp.concatenate([own[tap + dz], other[tap + dz]], axis=0) for dz in range(3)],
                    axis=1,
                )
                term = lax.dot_general(left, right, NT, preferred_element_type=jnp.float32)
                total = term if total is None else total + term
        total = total + bias
        low, high = (total[: quad * rows], total[quad * rows :])
        lane = lax.broadcasted_iota(jnp.int32, low.shape, 1)
        out[q, 0] = jnp.where(lane < swap, low, pltpu.roll(high, swap, 1)).astype(jnp.bfloat16)
        out[q, 1] = jnp.where(lane < swap, pltpu.roll(low, swap, 1), high).astype(jnp.bfloat16)


def first_conv(mine, theirs, own, near, far, held, planes):
    cells, half = mine.shape
    rows = cells // planes
    return pl.pallas_call(
        first_kernel,
        out_shape=jax.ShapeDtypeStruct((2, 2, cells // 4, half), jnp.bfloat16),
        in_specs=[pl.BlockSpec(memory_space=pltpu.VMEM)] * 6,
        out_specs=pl.BlockSpec(memory_space=pltpu.VMEM),
        scratch_shapes=[
            pltpu.VMEM((planes + 2, rows, 3 * half), jnp.bfloat16),
            pltpu.VMEM((planes + 2, rows + 16, 3 * half), jnp.bfloat16),
        ],
        compiler_params=pltpu.CompilerParams(vmem_limit_bytes=32 * 2**20),
    )(mine, theirs, own, near, far, held)


def second_kernel(hidden, own, other, held, out, even, odd):
    planes = even.shape[0] - 2
    rows, width = even.shape[1:]
    lanes = hidden.shape[2]
    k = lanes // 2
    swap = lanes // 2
    d = lax.axis_index("dp")
    blank = jnp.zeros((1,) + odd.shape[1:], odd.dtype)
    odd[0:1] = blank
    odd[planes + 1 : planes + 2] = blank
    even[0:1] = blank[:, :rows]
    even[planes + 1 : planes + 2] = blank[:, :rows]
    cell = lax.broadcasted_iota(jnp.int32, (rows, lanes), 0) % 8
    lane = lax.broadcasted_iota(jnp.int32, (rows, lanes), 1)
    low = lane < swap
    edge = jnp.zeros((8, width), jnp.float32)
    per = hidden.shape[1] // rows
    for q in range(2):
        for r in range(per):
            packed = hidden[q, r * rows : (r + 1) * rows].astype(jnp.float32)
            turned = pltpu.roll(packed, swap, 1)
            for u in range(2):
                here, there = (packed, turned) if u == 0 else (turned, packed)
                below = jnp.where(cell == 0, 0.0, pltpu.roll(here, 1, 0))
                above = jnp.where(cell == 7, 0.0, pltpu.roll(here, rows - 1, 0))
                taps = jnp.concatenate(
                    [jnp.where(low, below, there), jnp.where(low, above, 0.0)], axis=1
                )
                x = (q * 2 + u) * per + r
                even[x + 1] = taps.astype(jnp.bfloat16)
                odd[x + 1] = jnp.concatenate([edge, taps, edge], axis=0).astype(jnp.bfloat16)
    lane = lax.broadcasted_iota(jnp.int32, own.shape[1:], 1)
    low = lane < swap
    rights = []
    for tap in range(0, own.shape[0], 3):
        rows_in = []
        for dz in range(3):
            one = jnp.where(d == 0, own[tap + dz], other[tap + dz])
            two = jnp.where(d == 0, other[tap + dz], own[tap + dz])
            rows_in.append(jnp.where(low, one, pltpu.roll(two, swap, 1)))
            rows_in.append(jnp.where(low, pltpu.roll(one, swap, 1), two))
        rights.append(jnp.concatenate(rows_in, axis=0))
    for q in range(2):
        total = None
        for dx in range(3):
            for dy in range(3):
                at = pl.ds(q * planes // 2 + dx, planes // 2)
                if dy == 1:
                    left = even[at]
                else:
                    left = odd[at, pl.ds(8 * dy, rows)]
                left = left.reshape(planes // 2 * rows, width)[:, : 3 * k]
                right = rights[dx * 3 + dy]
                term = lax.dot_general(left, right, NN, preferred_element_type=jnp.float32)
                total = term if total is None else total + term
        total = total + held[2:3] * jnp.where(lax.axis_index("space") == 0, 1.0, 0.0)
        n = planes // 2 * rows
        out[q * n : (q + 1) * n] = total.astype(jnp.bfloat16)


def second_conv(hidden, own, other, held, planes):
    _, rows2, lanes = hidden.shape
    cells = rows2 * 4
    rows = cells // planes
    return pl.pallas_call(
        second_kernel,
        out_shape=jax.ShapeDtypeStruct((cells, lanes), jnp.bfloat16),
        in_specs=[pl.BlockSpec(memory_space=pltpu.VMEM)] * 4,
        out_specs=pl.BlockSpec(memory_space=pltpu.VMEM),
        scratch_shapes=[
            pltpu.VMEM((planes + 2, rows, 2 * lanes), jnp.bfloat16),
            pltpu.VMEM((planes + 2, rows + 16, 2 * lanes), jnp.bfloat16),
        ],
        compiler_params=pltpu.CompilerParams(vmem_limit_bytes=32 * 2**20),
    )(hidden, own, other, held)


def stationary(
    coarse, skip, up_weight, up_bias, first_weight, first_bias, second_weight, second_bias
):
    s, d, c = (lax.axis_index(a) for a in ("space", "dp", "chan"))
    group = ("space", "dp", "chan")
    _, _, cx, cy, cin = coarse.shape
    _, bx, fy, fz, half = skip.shape
    fx = 4 * bx
    cells = cx * cy
    block = bx * fy * fz
    taps, kb, _, own_n = up_weight.shape
    up_rows = taps * own_n
    first_own = first_weight[:, :, 0, :].transpose(0, 2, 1)
    up_rows_own = up_weight[:, :, 0, :].transpose(0, 2, 1).reshape(up_rows, kb)
    early, late, near, held = packed(
        up_rows_own,
        coarse.reshape(cells, cin),
        skip.reshape(block, half),
        first_own,
        [bias.reshape(1, half) for bias in (up_bias, first_bias, second_bias)],
    )
    early_route, late_route, cross_route = line_routes()
    late = lax.ppermute(late, group, late_route)
    late_other = swapped(late[:up_rows], "dp")
    early = lax.ppermute(early, group, early_route)
    early_other = lax.ppermute(up_rows_own, group, cross_route)
    near = swapped(near, "dp")
    late_other, early, early_other = lax.optimization_barrier((late_other, early, early_other))
    far = swapped(near, "groups")
    second_raw, late = lax.optimization_barrier((second_weight[:, :, 0, :], late))
    second_own = dense(second_raw)
    second_own, late_other = lax.optimization_barrier((second_own, late_other))
    second_other = swapped(second_own, "dp")
    slabs = swapped(jnp.stack([early[up_rows:], late[up_rows:]]), "chan")
    part = up_part(early, late, early_other, late_other, slabs, held, fx * fy * fz)
    part, far = lax.optimization_barrier((part, far))
    first = first_conv(part, swapped(part, "chan"), first_own, near, far, held, fx)
    mine = lax.dynamic_index_in_dim(first, c, 0, keepdims=False)
    theirs = lax.dynamic_index_in_dim(first, 1 - c, 0, keepdims=False)
    chunks = jnp.stack([mine, swapped(theirs, "chan")]).reshape(4, block, half)

    def chunk_for(plane):
        place = 2 * ((plane // 2) ^ c) + ((plane % 2) ^ d)
        return lax.dynamic_index_in_dim(chunks, place, 0, keepdims=False)

    hidden = jax.nn.silu(reduced(chunk_for, s)).astype(jnp.bfloat16)
    hidden, second_other = lax.optimization_barrier((hidden, second_other))
    hidden = ordered(c, hidden, swapped(hidden, "chan"), 0)
    second = second_conv(hidden, second_own, second_other, held, fx).reshape(4, block, half)
    total = reduced(lambda plane: lax.dynamic_index_in_dim(second, plane, 0, keepdims=False), s)
    return total.astype(jnp.bfloat16).reshape(skip.shape)


def keeps_weights(mesh):
    sizes = tuple(mesh.shape[a] for a in ("groups", "space", "dp", "chan"))
    return sizes == (2, 4, 2, 2)


def solution(mesh):
    return jax.shard_map(
        stationary if keeps_weights(mesh) else body,
        mesh=mesh,
        in_specs=(
            P(("groups", "dp"), "space", None, None, None),
            P(("groups", "dp"), "space", None, None, "chan"),
            P(None, "space", "chan", "dp"),
            P("chan"),
            P(None, "space", "chan", "dp"),
            P("chan"),
            P(None, "space", "chan", "dp"),
            P("chan"),
        ),
        out_specs=P(("groups", "dp"), "space", None, None, "chan"),
        check_vma=False,
    )
```

```python
import jax
import jax.numpy as jnp
from jax import lax
from jax.experimental import pallas as pl
from jax.experimental.pallas import tpu as pltpu
from jax.sharding import PartitionSpec as P


def padded_2(array, sides, width):
    for axis, dim in sides:
        peers, length = (lax.axis_size(axis), array.shape[dim])
        up = [(i, (i + 1) % peers) for i in range(peers - 1)]
        down = [(j, i) for i, j in up]
        last = lax.slice_in_dim(array, length - width, length, axis=dim)
        first = lax.slice_in_dim(array, 0, width, axis=dim)
        before = lax.ppermute(last, axis, up)
        after = lax.ppermute(first, axis, down)
        array = jnp.concatenate([before, array, after], axis=dim)
    return array


def alternate(total, bias):
    samples, depth_cells, width_cells, height_cells, taps, outputs = total.shape
    grid = total.reshape(samples, depth_cells, width_cells, height_cells, 2, 2, 2, outputs)
    grid = grid.transpose(0, 2, 4, 3, 5, 1, 6, 7)
    grid = grid.reshape(samples, 2 * width_cells, 2 * height_cells, 2 * depth_cells, outputs)
    return (grid + bias).astype(jnp.bfloat16)


def upsample_block(coarse, up_weight):
    columns = lax.all_gather(up_weight, "dp", axis=3, tiled=True)[:, :, 0, :]
    initial = jnp.zeros(coarse.shape[:4] + (8, columns.shape[2]), jnp.float32)

    def accumulate(summed, weight_rows, offset):
        return jnp.einsum(
            "szxyi,kio->szxyko", coarse, weight_rows, preferred_element_type=jnp.float32
        )

    return accumulate(initial, lax.all_gather(columns, "space", axis=1, tiled=True), jnp.int32(0))


def spatial_conv(padded, weight_block):
    kernel = weight_block.reshape(3, 3, 3, weight_block.shape[1], weight_block.shape[2])
    return lax.conv_general_dilated(
        padded,
        kernel,
        (1, 1, 1),
        [(0, 0), (1, 1), (1, 1)],
        dimension_numbers=("NDHWC", "DHWIO", "NDHWC"),
        preferred_element_type=jnp.float32,
    )


def folded_conv(padded, columns, base_shape):
    initial = jnp.zeros(base_shape + (columns.shape[2],), jnp.float32)

    def accumulate(summed, weight_rows, offset):
        sliced = lax.dynamic_slice_in_dim(padded, offset, weight_rows.shape[1], 4)
        return summed + spatial_conv(sliced, weight_rows)

    return (accumulate, initial)


def body(coarse, skip, up_weight, up_bias, first_weight, first_bias, second_weight, second_bias):
    slabs = lax.all_to_all(coarse, "space", split_axis=2, concat_axis=1, tiled=True)
    upsampled = alternate(upsample_block(slabs, up_weight), up_bias)
    up_full, skip_full = (
        lax.all_gather(upsampled, "chan", axis=4, tiled=True),
        lax.all_gather(skip, "chan", axis=4, tiled=True),
    )
    joined = jnp.concatenate([up_full, skip_full], axis=4)
    padded = padded_2(joined, (("space", 1),), 1)
    base_shape = joined.shape[:4]
    first_columns = lax.all_gather(first_weight, "dp", axis=3, tiled=True)[:, :, 0, :]
    accumulate, initial = folded_conv(padded, first_columns, base_shape)
    first = accumulate(
        initial, lax.all_gather(first_columns, "space", axis=1, tiled=True), jnp.int32(0)
    )
    hidden = jax.nn.silu(first + first_bias).astype(jnp.bfloat16)
    hidden_full = lax.all_gather(hidden, "chan", axis=4, tiled=True)
    hidden_padded = padded_2(hidden_full, (("space", 1),), 1)
    second_columns = lax.all_gather(second_weight, "dp", axis=3, tiled=True)[:, :, 0, :]
    accumulate_two, initial_two = folded_conv(hidden_padded, second_columns, base_shape)
    second = accumulate_two(
        initial_two, lax.all_gather(second_columns, "space", axis=1, tiled=True), jnp.int32(0)
    )
    return (second + second_bias).astype(jnp.bfloat16)


def swapped(array, axis):
    return lax.ppermute(array, axis, [(0, 1), (1, 0)])


def ordered(index, own, other, axis=0):
    first = jnp.where(index == 0, own, other)
    second = jnp.where(index == 0, other, own)
    return jnp.stack([first, second], axis=axis)


def pack_kernel(weight, coarse, skip, first, biases, early, late, half, held, sems):
    s = lax.axis_index("space")
    g = lax.axis_index("groups")
    kb = early.shape[1]
    rows, deep = (weight.shape[0], coarse.shape[0])
    span = half.shape[0]

    def fill(up_packet, skip_packet):
        moves = [(weight, up_packet.at[pl.ds(0, rows)])]
        for i in range(coarse.shape[1] // kb):
            place = up_packet.at[pl.ds(rows + i * deep, deep)]
            moves.append((coarse.at[:, pl.ds(i * kb, kb)], place))
        moves.append((skip, skip_packet.at[pl.ds(0, skip.shape[0])]))
        rest = skip_packet.shape[0] - skip.shape[0]
        moves.append((weight.at[pl.ds(0, rest)], skip_packet.at[pl.ds(skip.shape[0], rest)]))
        moves.append((first.at[pl.ds(g * (first.shape[0] - span), span)], half))
        for i, bias in enumerate(biases):
            moves.append((bias, held.at[pl.ds(i, 1)]))
        copies = [
            pltpu.make_async_copy(source, place, sems.at[i])
            for i, (source, place) in enumerate(moves)
        ]
        for copy in copies:
            copy.start()
        for copy in copies:
            copy.wait()

    @pl.when(s < 2)
    def _():
        fill(early, late)

    @pl.when(s >= 2)
    def _():
        fill(late, early)


def packed(weight, coarse, skip, first, biases):
    rows, kb = weight.shape
    deep, cin = coarse.shape
    count = len(biases)
    packet = jax.ShapeDtypeStruct((rows + deep * (cin // kb), kb), jnp.bfloat16)
    span = (first.shape[0] + 1) // 2
    half = jax.ShapeDtypeStruct((span,) + first.shape[1:], jnp.bfloat16)
    held = jax.ShapeDtypeStruct((count,) + biases[0].shape[1:], jnp.float32)

    def kernel(*refs):
        pack_kernel(*refs[:4], refs[4 : 4 + count], *refs[4 + count :])

    return pl.pallas_call(
        kernel,
        out_shape=(packet, packet, half, held),
        in_specs=[pl.BlockSpec(memory_space=pltpu.HBM)] * (4 + count),
        out_specs=[pl.BlockSpec(memory_space=pltpu.VMEM)] * 4,
        scratch_shapes=[pltpu.SemaphoreType.DMA((4 + cin // kb + count,))],
        compiler_params=pltpu.CompilerParams(vmem_limit_bytes=60 * 2**20),
    )(weight, coarse, skip, first, *biases)


def dense_kernel(weight, out):
    deep = weight.shape[1] // 2
    for tap in range(weight.shape[0]):
        out[tap] = jnp.concatenate([weight[tap, :deep], weight[tap, deep:]], axis=1)


def dense(weight):
    taps, rows, lanes = weight.shape
    return pl.pallas_call(
        dense_kernel,
        out_shape=jax.ShapeDtypeStruct((taps, rows // 2, 2 * lanes), weight.dtype),
        in_specs=[pl.BlockSpec(memory_space=pltpu.VMEM)],
        out_specs=pl.BlockSpec(memory_space=pltpu.VMEM),
        compiler_params=pltpu.CompilerParams(vmem_limit_bytes=16 * 2**20),
    )(weight)


def up_kernel(early, late, early_other, late_other, slabs, held, part):
    s, d, c = (lax.axis_index(a) for a in ("space", "dp", "chan"))
    rows, kb = early_other.shape
    deep = slabs.shape[1] // 4
    taps = 8
    own_n = rows // taps
    half = part.shape[1]
    all_cells = part.shape[0] - 8
    block = all_cells // 4
    part[pl.ds(all_cells, 8)] = jnp.broadcast_to(held[1:2], (8, half))

    @pl.when(s < 2)
    def _():
        lefts, rights = ([], [])
        for k in range(2):
            pieces = []
            for parity in range(2):
                for i, packet in enumerate((early, late)):
                    low = packet[pl.ds(rows + 2 * k * deep, deep)]
                    high = packet[pl.ds(rows + (2 * k + 1) * deep, deep)]
                    mine = jnp.where(c == 0, low, high)
                    low = slabs[i, pl.ds(2 * k * deep, deep)]
                    high = slabs[i, pl.ds((2 * k + 1) * deep, deep)]
                    theirs = jnp.where(c == 0, low, high)
                    pieces.append(jnp.where(c == parity, mine, theirs))
            lefts.append(jnp.concatenate(pieces, axis=0))
            packet, other = ((early, early_other), (late, late_other))[k]
            pieces = []
            for tap in range(taps):
                one = packet[pl.ds(tap * own_n, own_n)]
                two = other[pl.ds(tap * own_n, own_n)]
                pieces += [jnp.where(d == 0, one, two), jnp.where(d == 0, two, one)]
            rights.append(jnp.concatenate(pieces, axis=0))
        left = jnp.concatenate(lefts, axis=1)
        right = jnp.concatenate(rights, axis=1)
        bias = held[0:1] * jnp.where(c == s, 1.0, 0.0)
        for tap in range(taps):
            a, b, cc = (tap // 4, tap // 2 % 2, tap % 2)
            total = lax.dot_general(
                left,
                right[tap * 2 * own_n : (tap + 1) * 2 * own_n],
                NT,
                preferred_element_type=jnp.float32,
            )
            total = total + bias
            for parity in range(2):
                for i in range(2):
                    z = 2 * (parity + 2 * i) + cc
                    for x in range(deep // 8):
                        at = (parity * 2 + i) * deep + x * 8
                        start = ((2 * x + a) * 16 + b) * 8 + z
                        part[pl.ds(start, 8, 16)] = total[at : at + 8]

    @pl.when(s >= 2)
    def _():
        for i, packet in enumerate((late, early)):
            values = packet[pl.ds(0, block)].astype(jnp.float32)
            for parity in range(2):
                place = pl.ds((2 * i + parity) * block, block)
                part[place] = jnp.where(c == parity, values, 0.0)


def up_part(early, late, early_other, late_other, slabs, held, cells):
    return pl.pallas_call(
        up_kernel,
        out_shape=jax.ShapeDtypeStruct((cells + 8, held.shape[1]), jnp.float32),
        in_specs=[pl.BlockSpec(memory_space=pltpu.VMEM)] * 6,
        out_specs=pl.BlockSpec(memory_space=pltpu.VMEM),
        compiler_params=pltpu.CompilerParams(vmem_limit_bytes=32 * 2**20),
    )(early, late, early_other, late_other, slabs, held)


def terms_of(chunks):
    terms = []
    for step, chunk in chunks:
        terms.append(lax.ppermute(chunk, "space", [(i, i ^ step) for i in range(4)]))
    return terms


def summed(start, terms):
    for term in terms:
        start = start + term.astype(jnp.float32)
    return start


def pick(pair, index):
    return lax.dynamic_index_in_dim(pair, index, 0, keepdims=False)


def line_routes():
    early, late, cross = ([], [], [])
    for s in range(4):
        for d in range(2):
            for c in range(2):
                source = (s * 2 + d) * 2 + c
                up_target = (c * 2 + d) * 2 + s % 2
                skip_target = ((2 + c) * 2 + d) * 2 + s % 2
                early.append((source, up_target if s < 2 else skip_target))
                late.append((source, skip_target if s < 2 else up_target))
                if s < 2:
                    cross.append((source, (c * 2 + 1 - d) * 2 + s % 2))
    return early, late, cross


NT = (((1,), (1,)), ((), ()))
NN = (((1,), (0,)), ((), ()))


def build_taps(planes_of, even, odd):
    planes = even.shape[0] - 2
    rows, width = even.shape[1:]
    blank = jnp.zeros((1,) + odd.shape[1:], odd.dtype)
    odd[0:1] = blank
    odd[planes + 1 : planes + 2] = blank
    even[0:1] = blank[:, :rows]
    even[planes + 1 : planes + 2] = blank[:, :rows]
    edge = jnp.zeros((8, width), jnp.float32)
    for x, taps in planes_of():
        even[x + 1] = taps.astype(jnp.bfloat16)
        odd[x + 1] = jnp.concatenate([edge, taps, edge], axis=0).astype(jnp.bfloat16)


def half_product(q, even, odd, right_of, form):
    planes = even.shape[0] - 2
    rows = even.shape[1]
    total = None
    for dx in range(3):
        for dy in range(3):
            at = pl.ds(q * (planes // 2) + dx, planes // 2)
            left = even[at] if dy == 1 else odd[at, pl.ds(8 * dy, rows)]
            right = right_of(dx * 3 + dy)
            width = right.shape[1] if form is NT else right.shape[0]
            left = left.reshape(planes // 2 * rows, left.shape[2])[:, :width]
            term = lax.dot_general(left, right, form, preferred_element_type=jnp.float32)
            total = term if total is None else total + term
    return total


def first_right(own, near, far):
    g = lax.axis_index("groups")
    span, taps = (near.shape[0], own.shape[0])

    def other(tap):
        if tap < span:
            lower, upper = (near[tap], far[tap])
        else:
            lower, upper = (far[tap - taps + span], near[tap - taps + span])
        if tap == span - 1:
            upper = near[0]
        return jnp.where(g == 0, lower, upper)

    def right_of(group):
        tap = 3 * group
        return jnp.concatenate(
            [jnp.concatenate([own[tap + i], other(tap + i)], axis=0) for i in range(3)], axis=1
        )

    return right_of


def first_out(total, out, q):
    half = total.shape[1]
    swap = half // 2
    low, high = (total[: total.shape[0] // 2], total[total.shape[0] // 2 :])
    lane = lax.broadcasted_iota(jnp.int32, low.shape, 1)
    out[q, 0] = jnp.where(lane < swap, low, pltpu.roll(high, swap, 1)).astype(jnp.bfloat16)
    out[q, 1] = jnp.where(lane < swap, pltpu.roll(low, swap, 1), high).astype(jnp.bfloat16)


def first_kernel(mine, theirs, own, near, far, out, tile, even, odd):
    s, c = (lax.axis_index(a) for a in ("space", "chan"))
    rows = even.shape[1]
    half = mine.shape[1]
    cells = mine.shape[0] - 8
    cell = lax.broadcasted_iota(jnp.int32, (rows, half), 0) % 8

    def planes_of():
        for x in range(cells // rows):
            plane = mine[x * rows : (x + 1) * rows] + theirs[x * rows : (x + 1) * rows]
            plane = plane.astype(jnp.bfloat16).astype(jnp.float32)
            below = jnp.where(cell == 0, 0.0, pltpu.roll(plane, 1, 0))
            above = jnp.where(cell == 7, 0.0, pltpu.roll(plane, rows - 1, 0))
            yield x, jnp.concatenate([below, plane, above], axis=1)

    build_taps(planes_of, even, odd)
    right_of = first_right(own, near, far)
    for q in range(2):
        first_out(half_product(q, even, odd, right_of, NT), out, q)
    bias = jnp.where(s // 2 == c, mine[pl.ds(cells, 8)], theirs[pl.ds(cells, 8)])
    turned = pltpu.roll(bias, half // 2, 1)
    lane = lax.broadcasted_iota(jnp.int32, bias.shape, 1)
    tile[...] = jnp.where((lane < half // 2) == (s % 2 == 0), bias, turned)


def first_conv(mine, theirs, own, near, far, planes):
    cells, half = (mine.shape[0] - 8, mine.shape[1])
    rows = cells // planes
    return pl.pallas_call(
        first_kernel,
        out_shape=(
            jax.ShapeDtypeStruct((2, 2, cells // 4, half), jnp.bfloat16),
            jax.ShapeDtypeStruct((8, half), jnp.float32),
        ),
        in_specs=[pl.BlockSpec(memory_space=pltpu.VMEM)] * 5,
        out_specs=[pl.BlockSpec(memory_space=pltpu.VMEM)] * 2,
        scratch_shapes=[
            pltpu.VMEM((planes + 2, rows, 3 * half), jnp.bfloat16),
            pltpu.VMEM((planes + 2, rows + 16, 3 * half), jnp.bfloat16),
        ],
        compiler_params=pltpu.CompilerParams(vmem_limit_bytes=32 * 2**20),
    )(mine, theirs, own, near, far)


def second_far_kernel(hidden, own, other, held, out, tile, even, odd, rights):
    s, d = (lax.axis_index(a) for a in ("space", "dp"))
    rows = even.shape[1]
    lanes = hidden.shape[2]
    swap = lanes // 2
    cell = lax.broadcasted_iota(jnp.int32, (rows, lanes), 0) % 8
    low = lax.broadcasted_iota(jnp.int32, (rows, lanes), 1) < swap
    per = hidden.shape[1] // rows

    def planes_of():
        for q in range(2):
            for r in range(per):
                packed = hidden[q, r * rows : (r + 1) * rows].astype(jnp.float32)
                turned = pltpu.roll(packed, swap, 1)
                for u in range(2):
                    here, there = (packed, turned) if u == 0 else (turned, packed)
                    below = jnp.where(cell == 0, 0.0, pltpu.roll(here, 1, 0))
                    above = jnp.where(cell == 7, 0.0, pltpu.roll(here, rows - 1, 0))
                    taps = [jnp.where(low, below, there), jnp.where(low, above, 0.0)]
                    yield (q * 2 + u) * per + r, jnp.concatenate(taps, axis=1)

    build_taps(planes_of, even, odd)
    low = lax.broadcasted_iota(jnp.int32, own.shape[1:], 1) < swap
    for group in range(own.shape[0] // 3):
        pieces = []
        for tap in range(3 * group, 3 * group + 3):
            one = jnp.where(d == 0, own[tap], other[tap])
            two = jnp.where(d == 0, other[tap], own[tap])
            pieces.append(jnp.where(low, one, pltpu.roll(two, swap, 1)))
            pieces.append(jnp.where(low, pltpu.roll(one, swap, 1), two))
        rights[group] = jnp.concatenate(pieces, axis=0)
    total = half_product(1 - s // 2, even, odd, lambda group: rights[group], NN)
    out[...] = total.astype(jnp.bfloat16).reshape(out.shape)
    tile[...] = jnp.broadcast_to(held[2:3], tile.shape)


def second_near_kernel(even, odd, rights, out):
    s = lax.axis_index("space")
    total = half_product(s // 2, even, odd, lambda group: rights[group], NN)
    out[...] = total.astype(jnp.bfloat16).reshape(out.shape)


def second_far(hidden, own, other, held, planes):
    _, rows2, lanes = hidden.shape
    rows = rows2 * 4 // planes
    return pl.pallas_call(
        second_far_kernel,
        out_shape=(
            jax.ShapeDtypeStruct((2, rows2, lanes), jnp.bfloat16),
            jax.ShapeDtypeStruct((8, lanes), jnp.float32),
            jax.ShapeDtypeStruct((planes + 2, rows, 2 * lanes), jnp.bfloat16),
            jax.ShapeDtypeStruct((planes + 2, rows + 16, 2 * lanes), jnp.bfloat16),
            jax.ShapeDtypeStruct((9, 6 * own.shape[1], lanes), jnp.bfloat16),
        ),
        in_specs=[pl.BlockSpec(memory_space=pltpu.VMEM)] * 4,
        out_specs=[pl.BlockSpec(memory_space=pltpu.VMEM)] * 5,
        compiler_params=pltpu.CompilerParams(vmem_limit_bytes=32 * 2**20),
    )(hidden, own, other, held)


def second_near(even, odd, rights):
    planes, rows, _ = even.shape
    return pl.pallas_call(
        second_near_kernel,
        out_shape=jax.ShapeDtypeStruct(
            (2, (planes - 2) * rows // 4, rights.shape[2]), jnp.bfloat16
        ),
        in_specs=[pl.BlockSpec(memory_space=pltpu.VMEM)] * 3,
        out_specs=pl.BlockSpec(memory_space=pltpu.VMEM),
        compiler_params=pltpu.CompilerParams(vmem_limit_bytes=32 * 2**20),
    )(even, odd, rights)


def stationary(
    coarse, skip, up_weight, up_bias, first_weight, first_bias, second_weight, second_bias
):
    s, d, c = (lax.axis_index(a) for a in ("space", "dp", "chan"))
    group = ("space", "dp", "chan")
    _, _, cx, cy, cin = coarse.shape
    _, bx, fy, fz, half = skip.shape
    fx = 4 * bx
    cells = cx * cy
    block = bx * fy * fz
    taps, kb, _, own_n = up_weight.shape
    up_rows = taps * own_n
    first_own = first_weight[:, :, 0, :].transpose(0, 2, 1)
    up_rows_own = up_weight[:, :, 0, :].transpose(0, 2, 1).reshape(up_rows, kb)
    early, late, near, held = packed(
        up_rows_own,
        coarse.reshape(cells, cin),
        skip.reshape(block, half),
        first_own,
        [bias.reshape(1, half) for bias in (up_bias, first_bias, second_bias)],
    )
    early_route, late_route, cross_route = line_routes()
    late = lax.ppermute(late, group, late_route)
    late_other = swapped(late[:up_rows], "dp")
    early = lax.ppermute(early, group, early_route)
    early_other = lax.ppermute(up_rows_own, group, cross_route)
    near = swapped(near, "dp")
    late_other, early, early_other = lax.optimization_barrier((late_other, early, early_other))
    far = swapped(near, "groups")
    second_raw, late = lax.optimization_barrier((second_weight[:, :, 0, :], late))
    second_own = dense(second_raw)
    second_own, late_other = lax.optimization_barrier((second_own, late_other))
    second_other = swapped(second_own, "dp")
    slabs = swapped(jnp.stack([early[up_rows:], late[up_rows:]]), "chan")
    part = up_part(early, late, early_other, late_other, slabs, held, fx * fy * fz)
    part, far = lax.optimization_barrier((part, far))
    part_other = swapped(part, "chan")
    first, tile = first_conv(part, part_other, first_own, near, far, fx)
    mine, theirs = (pick(first, c), swapped(pick(first, 1 - c), "chan"))
    chunks = jnp.stack([mine, theirs]).reshape(4, block, half)

    def chunk_for(plane):
        return pick(chunks, 2 * ((plane // 2) ^ c) + ((plane % 2) ^ d))

    terms = terms_of([(step, chunk_for(s ^ step)) for step in (3, 2, 1)])
    terms[0], second_other = lax.optimization_barrier((terms[0], second_other))
    total = summed(chunk_for(s).astype(jnp.float32) + tile[:1], terms)
    hidden = jax.nn.silu(total).astype(jnp.bfloat16)
    hidden = ordered(c, hidden, swapped(hidden, "chan"), 0)
    away, tile, even, odd, rights = second_far(hidden, second_own, second_other, held, fx)
    sends = [(3, pick(away, (s + 1) % 2)), (2, pick(away, s % 2))]
    terms = terms_of(sends)
    even, sends = lax.optimization_barrier((even, sends))
    home = second_near(even, odd, rights)
    terms += terms_of([(1, pick(home, (s + 1) % 2))])
    total = summed(pick(home, s % 2).astype(jnp.float32) + tile[:1], terms)
    return total.astype(jnp.bfloat16).reshape(skip.shape)


def keeps_weights(mesh):
    sizes = tuple(mesh.shape[a] for a in ("groups", "space", "dp", "chan"))
    return sizes == (2, 4, 2, 2)


def solution(mesh):
    return jax.shard_map(
        stationary if keeps_weights(mesh) else body,
        mesh=mesh,
        in_specs=(
            P(("groups", "dp"), "space", None, None, None),
            P(("groups", "dp"), "space", None, None, "chan"),
            P(None, "space", "chan", "dp"),
            P("chan"),
            P(None, "space", "chan", "dp"),
            P("chan"),
            P(None, "space", "chan", "dp"),
            P("chan"),
        ),
        out_specs=P(("groups", "dp"), "space", None, None, "chan"),
        check_vma=False,
    )
```

```python
import jax
import jax.numpy as jnp
from jax import lax
from jax.experimental import pallas as pl
from jax.experimental.pallas import tpu as pltpu
from jax.sharding import PartitionSpec as P


def padded_2(array, sides, width):
    for axis, dim in sides:
        peers, length = (lax.axis_size(axis), array.shape[dim])
        up = [(i, (i + 1) % peers) for i in range(peers - 1)]
        down = [(j, i) for i, j in up]
        last = lax.slice_in_dim(array, length - width, length, axis=dim)
        first = lax.slice_in_dim(array, 0, width, axis=dim)
        before = lax.ppermute(last, axis, up)
        after = lax.ppermute(first, axis, down)
        array = jnp.concatenate([before, array, after], axis=dim)
    return array


def alternate(total, bias):
    samples, depth_cells, width_cells, height_cells, taps, outputs = total.shape
    grid = total.reshape(samples, depth_cells, width_cells, height_cells, 2, 2, 2, outputs)
    grid = grid.transpose(0, 2, 4, 3, 5, 1, 6, 7)
    grid = grid.reshape(samples, 2 * width_cells, 2 * height_cells, 2 * depth_cells, outputs)
    return (grid + bias).astype(jnp.bfloat16)


def upsample_block(coarse, up_weight):
    columns = lax.all_gather(up_weight, "dp", axis=3, tiled=True)[:, :, 0, :]
    initial = jnp.zeros(coarse.shape[:4] + (8, columns.shape[2]), jnp.float32)

    def accumulate(summed, weight_rows, offset):
        return jnp.einsum(
            "szxyi,kio->szxyko", coarse, weight_rows, preferred_element_type=jnp.float32
        )

    return accumulate(initial, lax.all_gather(columns, "space", axis=1, tiled=True), jnp.int32(0))


def spatial_conv(padded, weight_block):
    kernel = weight_block.reshape(3, 3, 3, weight_block.shape[1], weight_block.shape[2])
    return lax.conv_general_dilated(
        padded,
        kernel,
        (1, 1, 1),
        [(0, 0), (1, 1), (1, 1)],
        dimension_numbers=("NDHWC", "DHWIO", "NDHWC"),
        preferred_element_type=jnp.float32,
    )


def folded_conv(padded, columns, base_shape):
    initial = jnp.zeros(base_shape + (columns.shape[2],), jnp.float32)

    def accumulate(summed, weight_rows, offset):
        sliced = lax.dynamic_slice_in_dim(padded, offset, weight_rows.shape[1], 4)
        return summed + spatial_conv(sliced, weight_rows)

    return (accumulate, initial)


def body(coarse, skip, up_weight, up_bias, first_weight, first_bias, second_weight, second_bias):
    slabs = lax.all_to_all(coarse, "space", split_axis=2, concat_axis=1, tiled=True)
    upsampled = alternate(upsample_block(slabs, up_weight), up_bias)
    up_full, skip_full = (
        lax.all_gather(upsampled, "chan", axis=4, tiled=True),
        lax.all_gather(skip, "chan", axis=4, tiled=True),
    )
    joined = jnp.concatenate([up_full, skip_full], axis=4)
    padded = padded_2(joined, (("space", 1),), 1)
    base_shape = joined.shape[:4]
    first_columns = lax.all_gather(first_weight, "dp", axis=3, tiled=True)[:, :, 0, :]
    accumulate, initial = folded_conv(padded, first_columns, base_shape)
    first = accumulate(
        initial, lax.all_gather(first_columns, "space", axis=1, tiled=True), jnp.int32(0)
    )
    hidden = jax.nn.silu(first + first_bias).astype(jnp.bfloat16)
    hidden_full = lax.all_gather(hidden, "chan", axis=4, tiled=True)
    hidden_padded = padded_2(hidden_full, (("space", 1),), 1)
    second_columns = lax.all_gather(second_weight, "dp", axis=3, tiled=True)[:, :, 0, :]
    accumulate_two, initial_two = folded_conv(hidden_padded, second_columns, base_shape)
    second = accumulate_two(
        initial_two, lax.all_gather(second_columns, "space", axis=1, tiled=True), jnp.int32(0)
    )
    return (second + second_bias).astype(jnp.bfloat16)


def swapped(array, axis):
    return lax.ppermute(array, axis, [(0, 1), (1, 0)])


def ordered(index, own, other, axis=0):
    first = jnp.where(index == 0, own, other)
    second = jnp.where(index == 0, other, own)
    return jnp.stack([first, second], axis=axis)


def dense_kernel(weight, out):
    deep = weight.shape[1] // 2
    for tap in range(weight.shape[0]):
        out[tap] = jnp.concatenate([weight[tap, :deep], weight[tap, deep:]], axis=1)


def dense(weight):
    taps, rows, lanes = weight.shape
    return pl.pallas_call(
        dense_kernel,
        out_shape=jax.ShapeDtypeStruct((taps, rows // 2, 2 * lanes), weight.dtype),
        in_specs=[pl.BlockSpec(memory_space=pltpu.VMEM)],
        out_specs=pl.BlockSpec(memory_space=pltpu.VMEM),
        compiler_params=pltpu.CompilerParams(vmem_limit_bytes=16 * 2**20),
    )(weight)


def up_kernel(early, late, early_other, late_other, slabs, held, part):
    s, d, c = (lax.axis_index(a) for a in ("space", "dp", "chan"))
    rows, kb = early_other.shape
    deep = slabs.shape[1] // 4
    taps = 8
    own_n = rows // taps
    half = part.shape[1]
    all_cells = part.shape[0] - 8
    block = all_cells // 4
    part[pl.ds(all_cells, 8)] = jnp.broadcast_to(held[1:2], (8, half))

    @pl.when(s < 2)
    def _():
        lefts, rights = ([], [])
        for k in range(2):
            pieces = []
            for parity in range(2):
                for i, packet in enumerate((early, late)):
                    low = packet[pl.ds(rows + 2 * k * deep, deep)]
                    high = packet[pl.ds(rows + (2 * k + 1) * deep, deep)]
                    mine = jnp.where(c == 0, low, high)
                    low = slabs[i, pl.ds(2 * k * deep, deep)]
                    high = slabs[i, pl.ds((2 * k + 1) * deep, deep)]
                    theirs = jnp.where(c == 0, low, high)
                    pieces.append(jnp.where(c == parity, mine, theirs))
            lefts.append(jnp.concatenate(pieces, axis=0))
            packet, other = ((early, early_other), (late, late_other))[k]
            pieces = []
            for tap in range(taps):
                one = packet[pl.ds(tap * own_n, own_n)]
                two = other[pl.ds(tap * own_n, own_n)]
                pieces += [jnp.where(d == 0, one, two), jnp.where(d == 0, two, one)]
            rights.append(jnp.concatenate(pieces, axis=0))
        left = jnp.concatenate(lefts, axis=1)
        right = jnp.concatenate(rights, axis=1)
        bias = held[0:1] * jnp.where(c == s, 1.0, 0.0)
        for tap in range(taps):
            a, b, cc = (tap // 4, tap // 2 % 2, tap % 2)
            total = lax.dot_general(
                left,
                right[tap * 2 * own_n : (tap + 1) * 2 * own_n],
                NT,
                preferred_element_type=jnp.float32,
            )
            total = total + bias
            for parity in range(2):
                for i in range(2):
                    z = 2 * (parity + 2 * i) + cc
                    for x in range(deep // 8):
                        at = (parity * 2 + i) * deep + x * 8
                        start = ((2 * x + a) * 16 + b) * 8 + z
                        part[pl.ds(start, 8, 16)] = total[at : at + 8]

    @pl.when(s >= 2)
    def _():
        for i, packet in enumerate((late, early)):
            values = packet[pl.ds(0, block)].astype(jnp.float32)
            for parity in range(2):
                place = pl.ds((2 * i + parity) * block, block)
                part[place] = jnp.where(c == parity, values, 0.0)


def up_part(early, late, early_other, late_other, slabs, held, cells):
    return pl.pallas_call(
        up_kernel,
        out_shape=jax.ShapeDtypeStruct((cells + 8, held.shape[1]), jnp.float32),
        in_specs=[pl.BlockSpec(memory_space=pltpu.VMEM)] * 6,
        out_specs=pl.BlockSpec(memory_space=pltpu.VMEM),
        compiler_params=pltpu.CompilerParams(vmem_limit_bytes=32 * 2**20),
    )(early, late, early_other, late_other, slabs, held)


def terms_of(chunks):
    terms = []
    for step, chunk in chunks:
        terms.append(lax.ppermute(chunk, "space", [(i, i ^ step) for i in range(4)]))
    return terms


def summed(start, terms):
    for term in terms:
        start = start + term.astype(jnp.float32)
    return start


def pick(pair, index):
    return lax.dynamic_index_in_dim(pair, index, 0, keepdims=False)


def line_routes():
    early, late, cross = ([], [], [])
    for s in range(4):
        for d in range(2):
            for c in range(2):
                source = (s * 2 + d) * 2 + c
                up_target = (c * 2 + d) * 2 + s % 2
                skip_target = ((2 + c) * 2 + d) * 2 + s % 2
                early.append((source, up_target if s < 2 else skip_target))
                late.append((source, skip_target if s < 2 else up_target))
                if s < 2:
                    cross.append((source, (c * 2 + 1 - d) * 2 + s % 2))
    return early, late, cross


NT = (((1,), (1,)), ((), ()))
NN = (((1,), (0,)), ((), ()))


def build_taps(planes_of, even, odd):
    planes = even.shape[0] - 2
    rows, width = even.shape[1:]
    blank = jnp.zeros((1,) + odd.shape[1:], odd.dtype)
    odd[0:1] = blank
    odd[planes + 1 : planes + 2] = blank
    even[0:1] = blank[:, :rows]
    even[planes + 1 : planes + 2] = blank[:, :rows]
    edge = jnp.zeros((8, width), jnp.float32)
    for x, taps in planes_of():
        even[x + 1] = taps.astype(jnp.bfloat16)
        odd[x + 1] = jnp.concatenate([edge, taps, edge], axis=0).astype(jnp.bfloat16)


def half_product(q, even, odd, right_of, form):
    planes = even.shape[0] - 2
    rows = even.shape[1]
    total = None
    for dx in range(3):
        for dy in range(3):
            at = pl.ds(q * (planes // 2) + dx, planes // 2)
            left = even[at] if dy == 1 else odd[at, pl.ds(8 * dy, rows)]
            right = right_of(dx * 3 + dy)
            width = right.shape[1] if form is NT else right.shape[0]
            left = left.reshape(planes // 2 * rows, left.shape[2])[:, :width]
            term = lax.dot_general(left, right, form, preferred_element_type=jnp.float32)
            total = term if total is None else total + term
    return total


def first_right(own, near, far):
    g = lax.axis_index("groups")
    span, taps = (near.shape[0], own.shape[0])

    def other(tap):
        if tap < span:
            lower, upper = (near[tap], far[tap])
        else:
            lower, upper = (far[tap - taps + span], near[tap - taps + span])
        if tap == span - 1:
            upper = near[0]
        return jnp.where(g == 0, lower, upper)

    def right_of(group):
        tap = 3 * group
        return jnp.concatenate(
            [jnp.concatenate([own[tap + i], other(tap + i)], axis=0) for i in range(3)], axis=1
        )

    return right_of


def first_out(total, out, q):
    half = total.shape[1]
    swap = half // 2
    low, high = (total[: total.shape[0] // 2], total[total.shape[0] // 2 :])
    lane = lax.broadcasted_iota(jnp.int32, low.shape, 1)
    out[q, 0] = jnp.where(lane < swap, low, pltpu.roll(high, swap, 1)).astype(jnp.bfloat16)
    out[q, 1] = jnp.where(lane < swap, pltpu.roll(low, swap, 1), high).astype(jnp.bfloat16)


def first_kernel(mine, theirs, own, near, far, out, tile, even, odd):
    s, c = (lax.axis_index(a) for a in ("space", "chan"))
    rows = even.shape[1]
    half = mine.shape[1]
    cells = mine.shape[0] - 8
    cell = lax.broadcasted_iota(jnp.int32, (rows, half), 0) % 8

    def planes_of():
        for x in range(cells // rows):
            plane = mine[x * rows : (x + 1) * rows] + theirs[x * rows : (x + 1) * rows]
            plane = plane.astype(jnp.bfloat16).astype(jnp.float32)
            below = jnp.where(cell == 0, 0.0, pltpu.roll(plane, 1, 0))
            above = jnp.where(cell == 7, 0.0, pltpu.roll(plane, rows - 1, 0))
            yield x, jnp.concatenate([below, plane, above], axis=1)

    build_taps(planes_of, even, odd)
    right_of = first_right(own, near, far)
    for q in range(2):
        first_out(half_product(q, even, odd, right_of, NT), out, q)
    bias = jnp.where(s // 2 == c, mine[pl.ds(cells, 8)], theirs[pl.ds(cells, 8)])
    turned = pltpu.roll(bias, half // 2, 1)
    lane = lax.broadcasted_iota(jnp.int32, bias.shape, 1)
    tile[...] = jnp.where((lane < half // 2) == (s % 2 == 0), bias, turned)


def first_conv(mine, theirs, own, near, far, planes):
    cells, half = (mine.shape[0] - 8, mine.shape[1])
    rows = cells // planes
    return pl.pallas_call(
        first_kernel,
        out_shape=(
            jax.ShapeDtypeStruct((2, 2, cells // 4, half), jnp.bfloat16),
            jax.ShapeDtypeStruct((8, half), jnp.float32),
        ),
        in_specs=[pl.BlockSpec(memory_space=pltpu.VMEM)] * 5,
        out_specs=[pl.BlockSpec(memory_space=pltpu.VMEM)] * 2,
        scratch_shapes=[
            pltpu.VMEM((planes + 2, rows, 3 * half), jnp.bfloat16),
            pltpu.VMEM((planes + 2, rows + 16, 3 * half), jnp.bfloat16),
        ],
        compiler_params=pltpu.CompilerParams(vmem_limit_bytes=32 * 2**20),
    )(mine, theirs, own, near, far)


def second_far_kernel(hidden, own, other, held, out, tile, even, odd, rights):
    s, d = (lax.axis_index(a) for a in ("space", "dp"))
    rows = even.shape[1]
    lanes = hidden.shape[2]
    swap = lanes // 2
    cell = lax.broadcasted_iota(jnp.int32, (rows, lanes), 0) % 8
    low = lax.broadcasted_iota(jnp.int32, (rows, lanes), 1) < swap
    per = hidden.shape[1] // rows

    def planes_of():
        for q in range(2):
            for r in range(per):
                packed = hidden[q, r * rows : (r + 1) * rows].astype(jnp.float32)
                turned = pltpu.roll(packed, swap, 1)
                for u in range(2):
                    here, there = (packed, turned) if u == 0 else (turned, packed)
                    below = jnp.where(cell == 0, 0.0, pltpu.roll(here, 1, 0))
                    above = jnp.where(cell == 7, 0.0, pltpu.roll(here, rows - 1, 0))
                    taps = [jnp.where(low, below, there), jnp.where(low, above, 0.0)]
                    yield (q * 2 + u) * per + r, jnp.concatenate(taps, axis=1)

    build_taps(planes_of, even, odd)
    low = lax.broadcasted_iota(jnp.int32, own.shape[1:], 1) < swap
    for group in range(own.shape[0] // 3):
        pieces = []
        for tap in range(3 * group, 3 * group + 3):
            one = jnp.where(d == 0, own[tap], other[tap])
            two = jnp.where(d == 0, other[tap], own[tap])
            pieces.append(jnp.where(low, one, pltpu.roll(two, swap, 1)))
            pieces.append(jnp.where(low, pltpu.roll(one, swap, 1), two))
        rights[group] = jnp.concatenate(pieces, axis=0)
    total = half_product(1 - s // 2, even, odd, lambda group: rights[group], NN)
    out[...] = total.astype(jnp.bfloat16).reshape(out.shape)
    tile[...] = jnp.broadcast_to(held[2:3], tile.shape)


def second_near_kernel(even, odd, rights, out):
    s = lax.axis_index("space")
    total = half_product(s // 2, even, odd, lambda group: rights[group], NN)
    out[...] = total.astype(jnp.bfloat16).reshape(out.shape)


def second_far(hidden, own, other, held, planes):
    _, rows2, lanes = hidden.shape
    rows = rows2 * 4 // planes
    return pl.pallas_call(
        second_far_kernel,
        out_shape=(
            jax.ShapeDtypeStruct((2, rows2, lanes), jnp.bfloat16),
            jax.ShapeDtypeStruct((8, lanes), jnp.float32),
            jax.ShapeDtypeStruct((planes + 2, rows, 2 * lanes), jnp.bfloat16),
            jax.ShapeDtypeStruct((planes + 2, rows + 16, 2 * lanes), jnp.bfloat16),
            jax.ShapeDtypeStruct((9, 6 * own.shape[1], lanes), jnp.bfloat16),
        ),
        in_specs=[pl.BlockSpec(memory_space=pltpu.VMEM)] * 4,
        out_specs=[pl.BlockSpec(memory_space=pltpu.VMEM)] * 5,
        compiler_params=pltpu.CompilerParams(vmem_limit_bytes=32 * 2**20),
    )(hidden, own, other, held)


def second_near(even, odd, rights):
    planes, rows, _ = even.shape
    return pl.pallas_call(
        second_near_kernel,
        out_shape=jax.ShapeDtypeStruct(
            (2, (planes - 2) * rows // 4, rights.shape[2]), jnp.bfloat16
        ),
        in_specs=[pl.BlockSpec(memory_space=pltpu.VMEM)] * 3,
        out_specs=pl.BlockSpec(memory_space=pltpu.VMEM),
        compiler_params=pltpu.CompilerParams(vmem_limit_bytes=32 * 2**20),
    )(even, odd, rights)


def stationary(
    coarse, skip, up_weight, up_bias, first_weight, first_bias, second_weight, second_bias
):
    s, d, c = (lax.axis_index(a) for a in ("space", "dp", "chan"))
    group = ("space", "dp", "chan")
    _, _, cx, cy, cin = coarse.shape
    _, bx, fy, fz, half = skip.shape
    fx = 4 * bx
    cells = cx * cy
    block = bx * fy * fz
    taps, kb, _, own_n = up_weight.shape
    up_rows = taps * own_n
    first_own = first_weight[:, :, 0, :].transpose(0, 2, 1)
    up_rows_own = up_weight[:, :, 0, :].transpose(0, 2, 1).reshape(up_rows, kb)
    columns = coarse.reshape(cells, cin)
    columns = [columns[:, i : i + kb] for i in range(0, cin, kb)]
    up_packet = jnp.concatenate([up_rows_own] + columns, axis=0)
    skip_rows = skip.reshape(block, half)
    skip_packet = jnp.pad(skip_rows, ((0, up_packet.shape[0] - block), (0, 0)))
    early = jnp.where(s < 2, up_packet, skip_packet)
    late = jnp.where(s < 2, skip_packet, up_packet)
    span = (first_own.shape[0] + 1) // 2
    start = lax.axis_index("groups") * (first_own.shape[0] - span)
    near = lax.dynamic_slice_in_dim(first_own, start, span, 0)
    held = jnp.stack([up_bias, first_bias, second_bias])
    early_route, late_route, cross_route = line_routes()
    late = lax.ppermute(late, group, late_route)
    late_other = swapped(late[:up_rows], "dp")
    early = lax.ppermute(early, group, early_route)
    early_other = lax.ppermute(up_rows_own, group, cross_route)
    near = swapped(near, "dp")
    late_other, early, early_other = lax.optimization_barrier((late_other, early, early_other))
    far = swapped(near, "groups")
    second_raw, late = lax.optimization_barrier((second_weight[:, :, 0, :], late))
    second_own = dense(second_raw)
    second_own, late_other = lax.optimization_barrier((second_own, late_other))
    second_other = swapped(second_own, "dp")
    slabs = swapped(jnp.stack([early[up_rows:], late[up_rows:]]), "chan")
    part = up_part(early, late, early_other, late_other, slabs, held, fx * fy * fz)
    part, far = lax.optimization_barrier((part, far))
    part_other = swapped(part, "chan")
    first, tile = first_conv(part, part_other, first_own, near, far, fx)
    mine, theirs = (pick(first, c), swapped(pick(first, 1 - c), "chan"))
    chunks = jnp.stack([mine, theirs]).reshape(4, block, half)

    def chunk_for(plane):
        return pick(chunks, 2 * ((plane // 2) ^ c) + ((plane % 2) ^ d))

    terms = terms_of([(step, chunk_for(s ^ step)) for step in (3, 2, 1)])
    terms[0], second_other = lax.optimization_barrier((terms[0], second_other))
    total = summed(chunk_for(s).astype(jnp.float32) + tile[:1], terms)
    hidden = jax.nn.silu(total).astype(jnp.bfloat16)
    hidden = ordered(c, hidden, swapped(hidden, "chan"), 0)
    away, tile, even, odd, rights = second_far(hidden, second_own, second_other, held, fx)
    sends = [(3, pick(away, (s + 1) % 2)), (2, pick(away, s % 2))]
    terms = terms_of(sends)
    even, sends = lax.optimization_barrier((even, sends))
    home = second_near(even, odd, rights)
    terms += terms_of([(1, pick(home, (s + 1) % 2))])
    total = summed(pick(home, s % 2).astype(jnp.float32) + tile[:1], terms)
    return total.astype(jnp.bfloat16).reshape(skip.shape)


def keeps_weights(mesh):
    sizes = tuple(mesh.shape[a] for a in ("groups", "space", "dp", "chan"))
    return sizes == (2, 4, 2, 2)


def solution(mesh):
    return jax.shard_map(
        stationary if keeps_weights(mesh) else body,
        mesh=mesh,
        in_specs=(
            P(("groups", "dp"), "space", None, None, None),
            P(("groups", "dp"), "space", None, None, "chan"),
            P(None, "space", "chan", "dp"),
            P("chan"),
            P(None, "space", "chan", "dp"),
            P("chan"),
            P(None, "space", "chan", "dp"),
            P("chan"),
        ),
        out_specs=P(("groups", "dp"), "space", None, None, "chan"),
        check_vma=False,
    )
```

```python
import jax
import jax.numpy as jnp
from jax import lax
from jax.experimental import pallas as pl
from jax.experimental.pallas import tpu as pltpu
from jax.sharding import PartitionSpec as P


def padded_2(array, sides, width):
    for axis, dim in sides:
        peers, length = (lax.axis_size(axis), array.shape[dim])
        up = [(i, (i + 1) % peers) for i in range(peers - 1)]
        down = [(j, i) for i, j in up]
        last = lax.slice_in_dim(array, length - width, length, axis=dim)
        first = lax.slice_in_dim(array, 0, width, axis=dim)
        before = lax.ppermute(last, axis, up)
        after = lax.ppermute(first, axis, down)
        array = jnp.concatenate([before, array, after], axis=dim)
    return array


def alternate(total, bias):
    samples, depth_cells, width_cells, height_cells, taps, outputs = total.shape
    grid = total.reshape(samples, depth_cells, width_cells, height_cells, 2, 2, 2, outputs)
    grid = grid.transpose(0, 2, 4, 3, 5, 1, 6, 7)
    grid = grid.reshape(samples, 2 * width_cells, 2 * height_cells, 2 * depth_cells, outputs)
    return (grid + bias).astype(jnp.bfloat16)


def upsample_block(coarse, up_weight):
    columns = lax.all_gather(up_weight, "dp", axis=3, tiled=True)[:, :, 0, :]
    initial = jnp.zeros(coarse.shape[:4] + (8, columns.shape[2]), jnp.float32)

    def accumulate(summed, weight_rows, offset):
        return jnp.einsum(
            "szxyi,kio->szxyko", coarse, weight_rows, preferred_element_type=jnp.float32
        )

    return accumulate(initial, lax.all_gather(columns, "space", axis=1, tiled=True), jnp.int32(0))


def spatial_conv(padded, weight_block):
    kernel = weight_block.reshape(3, 3, 3, weight_block.shape[1], weight_block.shape[2])
    return lax.conv_general_dilated(
        padded,
        kernel,
        (1, 1, 1),
        [(0, 0), (1, 1), (1, 1)],
        dimension_numbers=("NDHWC", "DHWIO", "NDHWC"),
        preferred_element_type=jnp.float32,
    )


def folded_conv(padded, columns, base_shape):
    initial = jnp.zeros(base_shape + (columns.shape[2],), jnp.float32)

    def accumulate(summed, weight_rows, offset):
        sliced = lax.dynamic_slice_in_dim(padded, offset, weight_rows.shape[1], 4)
        return summed + spatial_conv(sliced, weight_rows)

    return (accumulate, initial)


def body(coarse, skip, up_weight, up_bias, first_weight, first_bias, second_weight, second_bias):
    slabs = lax.all_to_all(coarse, "space", split_axis=2, concat_axis=1, tiled=True)
    upsampled = alternate(upsample_block(slabs, up_weight), up_bias)
    up_full, skip_full = (
        lax.all_gather(upsampled, "chan", axis=4, tiled=True),
        lax.all_gather(skip, "chan", axis=4, tiled=True),
    )
    joined = jnp.concatenate([up_full, skip_full], axis=4)
    padded = padded_2(joined, (("space", 1),), 1)
    base_shape = joined.shape[:4]
    first_columns = lax.all_gather(first_weight, "dp", axis=3, tiled=True)[:, :, 0, :]
    accumulate, initial = folded_conv(padded, first_columns, base_shape)
    first = accumulate(
        initial, lax.all_gather(first_columns, "space", axis=1, tiled=True), jnp.int32(0)
    )
    hidden = jax.nn.silu(first + first_bias).astype(jnp.bfloat16)
    hidden_full = lax.all_gather(hidden, "chan", axis=4, tiled=True)
    hidden_padded = padded_2(hidden_full, (("space", 1),), 1)
    second_columns = lax.all_gather(second_weight, "dp", axis=3, tiled=True)[:, :, 0, :]
    accumulate_two, initial_two = folded_conv(hidden_padded, second_columns, base_shape)
    second = accumulate_two(
        initial_two, lax.all_gather(second_columns, "space", axis=1, tiled=True), jnp.int32(0)
    )
    return (second + second_bias).astype(jnp.bfloat16)


def swapped(array, axis):
    return lax.ppermute(array, axis, [(0, 1), (1, 0)])


def ordered(index, own, other, axis=0):
    first = jnp.where(index == 0, own, other)
    second = jnp.where(index == 0, other, own)
    return jnp.stack([first, second], axis=axis)


def dense_kernel(weight, out):
    deep = weight.shape[1] // 2
    for tap in range(weight.shape[0]):
        out[tap] = jnp.concatenate([weight[tap, :deep], weight[tap, deep:]], axis=1)


def dense(weight):
    taps, rows, lanes = weight.shape
    return pl.pallas_call(
        dense_kernel,
        out_shape=jax.ShapeDtypeStruct((taps, rows // 2, 2 * lanes), weight.dtype),
        in_specs=[pl.BlockSpec(memory_space=pltpu.VMEM)],
        out_specs=pl.BlockSpec(memory_space=pltpu.VMEM),
        compiler_params=pltpu.CompilerParams(vmem_limit_bytes=16 * 2**20),
    )(weight)


def up_kernel(early, late, early_other, late_other, slabs, held, part):
    s, d, c = (lax.axis_index(a) for a in ("space", "dp", "chan"))
    rows, kb = early_other.shape
    deep = slabs.shape[1] // 4
    taps = 8
    own_n = rows // taps
    half = part.shape[1]
    all_cells = part.shape[0] - 8
    block = all_cells // 4
    part[pl.ds(all_cells, 8)] = jnp.broadcast_to(held[1:2], (8, half))

    @pl.when(s < 2)
    def _():
        lefts, rights = ([], [])
        for k in range(2):
            pieces = []
            for parity in range(2):
                for i, packet in enumerate((early, late)):
                    low = packet[pl.ds(rows + 2 * k * deep, deep)]
                    high = packet[pl.ds(rows + (2 * k + 1) * deep, deep)]
                    mine = jnp.where(c == 0, low, high)
                    low = slabs[i, pl.ds(2 * k * deep, deep)]
                    high = slabs[i, pl.ds((2 * k + 1) * deep, deep)]
                    theirs = jnp.where(c == 0, low, high)
                    pieces.append(jnp.where(c == parity, mine, theirs))
            lefts.append(jnp.concatenate(pieces, axis=0))
            packet, other = ((early, early_other), (late, late_other))[k]
            pieces = []
            for tap in range(taps):
                one = packet[pl.ds(tap * own_n, own_n)]
                two = other[pl.ds(tap * own_n, own_n)]
                pieces += [jnp.where(d == 0, one, two), jnp.where(d == 0, two, one)]
            rights.append(jnp.concatenate(pieces, axis=0))
        left = jnp.concatenate(lefts, axis=1)
        right = jnp.concatenate(rights, axis=1)
        bias = held[0:1] * jnp.where(c == s, 1.0, 0.0)
        for tap in range(taps):
            a, b, cc = (tap // 4, tap // 2 % 2, tap % 2)
            total = lax.dot_general(
                left,
                right[tap * 2 * own_n : (tap + 1) * 2 * own_n],
                NT,
                preferred_element_type=jnp.float32,
            )
            total = total + bias
            for parity in range(2):
                for i in range(2):
                    z = 2 * (parity + 2 * i) + cc
                    for x in range(deep // 8):
                        at = (parity * 2 + i) * deep + x * 8
                        start = ((2 * x + a) * 16 + b) * 8 + z
                        part[pl.ds(start, 8, 16)] = total[at : at + 8]

    @pl.when(s >= 2)
    def _():
        for i, packet in enumerate((late, early)):
            values = packet[pl.ds(0, block)].astype(jnp.float32)
            for parity in range(2):
                place = pl.ds((2 * i + parity) * block, block)
                part[place] = jnp.where(c == parity, values, 0.0)


def up_part(early, late, early_other, late_other, slabs, held, cells):
    return pl.pallas_call(
        up_kernel,
        out_shape=jax.ShapeDtypeStruct((cells + 8, held.shape[1]), jnp.float32),
        in_specs=[pl.BlockSpec(memory_space=pltpu.VMEM)] * 6,
        out_specs=pl.BlockSpec(memory_space=pltpu.VMEM),
        compiler_params=pltpu.CompilerParams(vmem_limit_bytes=32 * 2**20),
        cost_estimate=pl.CostEstimate(flops=1000, bytes_accessed=1000, transcendentals=0),
    )(early, late, early_other, late_other, slabs, held)


def terms_of(chunks):
    terms = []
    for step, chunk in chunks:
        terms.append(lax.ppermute(chunk, "space", [(i, i ^ step) for i in range(4)]))
    return terms


def summed(start, terms):
    for term in terms:
        start = start + term.astype(jnp.float32)
    return start


def pick(pair, index):
    return lax.dynamic_index_in_dim(pair, index, 0, keepdims=False)


def line_routes():
    early, late, cross = ([], [], [])
    for s in range(4):
        for d in range(2):
            for c in range(2):
                source = (s * 2 + d) * 2 + c
                up_target = (c * 2 + d) * 2 + s % 2
                skip_target = ((2 + c) * 2 + d) * 2 + s % 2
                early.append((source, up_target if s < 2 else skip_target))
                late.append((source, skip_target if s < 2 else up_target))
                if s < 2:
                    cross.append((source, (c * 2 + 1 - d) * 2 + s % 2))
    return early, late, cross


NT = (((1,), (1,)), ((), ()))
NN = (((1,), (0,)), ((), ()))


def build_taps(planes_of, even, odd):
    planes = even.shape[0] - 2
    rows, width = even.shape[1:]
    blank = jnp.zeros((1,) + odd.shape[1:], odd.dtype)
    odd[0:1] = blank
    odd[planes + 1 : planes + 2] = blank
    even[0:1] = blank[:, :rows]
    even[planes + 1 : planes + 2] = blank[:, :rows]
    edge = jnp.zeros((8, width), jnp.float32)
    for x, taps in planes_of():
        even[x + 1] = taps.astype(jnp.bfloat16)
        odd[x + 1] = jnp.concatenate([edge, taps, edge], axis=0).astype(jnp.bfloat16)


def half_product(q, even, odd, right_of, form):
    planes = even.shape[0] - 2
    rows = even.shape[1]
    total = None
    for dx in range(3):
        for dy in range(3):
            at = pl.ds(q * (planes // 2) + dx, planes // 2)
            left = even[at] if dy == 1 else odd[at, pl.ds(8 * dy, rows)]
            right = right_of(dx * 3 + dy)
            width = right.shape[1] if form is NT else right.shape[0]
            left = left.reshape(planes // 2 * rows, left.shape[2])[:, :width]
            term = lax.dot_general(left, right, form, preferred_element_type=jnp.float32)
            total = term if total is None else total + term
    return total


def other_kernel(near, far, out):
    g = lax.axis_index("groups")
    span, taps = (near.shape[0], out.shape[0])
    for tap in range(taps):
        if tap < span:
            lower, upper = (near[tap], far[tap])
        else:
            lower, upper = (far[tap - taps + span], near[tap - taps + span])
        if tap == span - 1:
            upper = near[0]
        out[tap] = jnp.where(g == 0, lower, upper)


def other_weights(near, far, taps):
    return pl.pallas_call(
        other_kernel,
        out_shape=jax.ShapeDtypeStruct((taps,) + near.shape[1:], near.dtype),
        in_specs=[pl.BlockSpec(memory_space=pltpu.VMEM)] * 2,
        out_specs=pl.BlockSpec(memory_space=pltpu.VMEM),
        compiler_params=pltpu.CompilerParams(vmem_limit_bytes=16 * 2**20),
        cost_estimate=pl.CostEstimate(flops=10000000000, bytes_accessed=0, transcendentals=0),
    )(near, far)


def first_right(own, other):
    def right_of(group):
        pairs = [jnp.concatenate([own[i], other[i]], axis=0) for i in range(3 * group, 3 * group + 3)]
        return jnp.concatenate(pairs, axis=1)

    return right_of


def first_out(total, out, q):
    half = total.shape[1]
    swap = half // 2
    low, high = (total[: total.shape[0] // 2], total[total.shape[0] // 2 :])
    lane = lax.broadcasted_iota(jnp.int32, low.shape, 1)
    out[q, 0] = jnp.where(lane < swap, low, pltpu.roll(high, swap, 1)).astype(jnp.bfloat16)
    out[q, 1] = jnp.where(lane < swap, pltpu.roll(low, swap, 1), high).astype(jnp.bfloat16)


def first_kernel(mine, theirs, own, other, out, tile, even, odd):
    s, c = (lax.axis_index(a) for a in ("space", "chan"))
    rows = even.shape[1]
    half = mine.shape[1]
    cells = mine.shape[0] - 8
    cell = lax.broadcasted_iota(jnp.int32, (rows, half), 0) % 8

    def planes_of():
        for x in range(cells // rows):
            plane = mine[x * rows : (x + 1) * rows] + theirs[x * rows : (x + 1) * rows]
            plane = plane.astype(jnp.bfloat16).astype(jnp.float32)
            below = jnp.where(cell == 0, 0.0, pltpu.roll(plane, 1, 0))
            above = jnp.where(cell == 7, 0.0, pltpu.roll(plane, rows - 1, 0))
            yield x, jnp.concatenate([below, plane, above], axis=1)

    build_taps(planes_of, even, odd)
    right_of = first_right(own, other)
    for q in range(2):
        first_out(half_product(q, even, odd, right_of, NT), out, q)
    bias = jnp.where(s // 2 == c, mine[pl.ds(cells, 8)], theirs[pl.ds(cells, 8)])
    turned = pltpu.roll(bias, half // 2, 1)
    lane = lax.broadcasted_iota(jnp.int32, bias.shape, 1)
    tile[...] = jnp.where((lane < half // 2) == (s % 2 == 0), bias, turned)


def first_conv(mine, theirs, own, other, planes):
    cells, half = (mine.shape[0] - 8, mine.shape[1])
    rows = cells // planes
    return pl.pallas_call(
        first_kernel,
        out_shape=(
            jax.ShapeDtypeStruct((2, 2, cells // 4, half), jnp.bfloat16),
            jax.ShapeDtypeStruct((8, half), jnp.float32),
        ),
        in_specs=[pl.BlockSpec(memory_space=pltpu.VMEM)] * 4,
        out_specs=[pl.BlockSpec(memory_space=pltpu.VMEM)] * 2,
        scratch_shapes=[
            pltpu.VMEM((planes + 2, rows, 3 * half), jnp.bfloat16),
            pltpu.VMEM((planes + 2, rows + 16, 3 * half), jnp.bfloat16),
        ],
        compiler_params=pltpu.CompilerParams(vmem_limit_bytes=32 * 2**20),
    )(mine, theirs, own, other)


def second_far_kernel(hidden, own, other, held, out, tile, even, odd, rights):
    s, d = (lax.axis_index(a) for a in ("space", "dp"))
    rows = even.shape[1]
    lanes = hidden.shape[2]
    swap = lanes // 2
    cell = lax.broadcasted_iota(jnp.int32, (rows, lanes), 0) % 8
    low = lax.broadcasted_iota(jnp.int32, (rows, lanes), 1) < swap
    per = hidden.shape[1] // rows

    def planes_of():
        for q in range(2):
            for r in range(per):
                packed = hidden[q, r * rows : (r + 1) * rows].astype(jnp.float32)
                turned = pltpu.roll(packed, swap, 1)
                for u in range(2):
                    here, there = (packed, turned) if u == 0 else (turned, packed)
                    below = jnp.where(cell == 0, 0.0, pltpu.roll(here, 1, 0))
                    above = jnp.where(cell == 7, 0.0, pltpu.roll(here, rows - 1, 0))
                    taps = [jnp.where(low, below, there), jnp.where(low, above, 0.0)]
                    yield (q * 2 + u) * per + r, jnp.concatenate(taps, axis=1)

    build_taps(planes_of, even, odd)
    low = lax.broadcasted_iota(jnp.int32, own.shape[1:], 1) < swap
    for group in range(own.shape[0] // 3):
        pieces = []
        for tap in range(3 * group, 3 * group + 3):
            one = jnp.where(d == 0, own[tap], other[tap])
            two = jnp.where(d == 0, other[tap], own[tap])
            pieces.append(jnp.where(low, one, pltpu.roll(two, swap, 1)))
            pieces.append(jnp.where(low, pltpu.roll(one, swap, 1), two))
        rights[group] = jnp.concatenate(pieces, axis=0)
    total = half_product(1 - s // 2, even, odd, lambda group: rights[group], NN)
    out[...] = total.astype(jnp.bfloat16).reshape(out.shape)
    tile[...] = jnp.broadcast_to(held[2:3], tile.shape)


def second_near_kernel(even, odd, rights, out):
    s = lax.axis_index("space")
    total = half_product(s // 2, even, odd, lambda group: rights[group], NN)
    out[...] = total.astype(jnp.bfloat16).reshape(out.shape)


def second_far(hidden, own, other, held, planes):
    _, rows2, lanes = hidden.shape
    rows = rows2 * 4 // planes
    return pl.pallas_call(
        second_far_kernel,
        out_shape=(
            jax.ShapeDtypeStruct((2, rows2, lanes), jnp.bfloat16),
            jax.ShapeDtypeStruct((8, lanes), jnp.float32),
            jax.ShapeDtypeStruct((planes + 2, rows, 2 * lanes), jnp.bfloat16),
            jax.ShapeDtypeStruct((planes + 2, rows + 16, 2 * lanes), jnp.bfloat16),
            jax.ShapeDtypeStruct((9, 6 * own.shape[1], lanes), jnp.bfloat16),
        ),
        in_specs=[pl.BlockSpec(memory_space=pltpu.VMEM)] * 4,
        out_specs=[pl.BlockSpec(memory_space=pltpu.VMEM)] * 5,
        compiler_params=pltpu.CompilerParams(vmem_limit_bytes=32 * 2**20),
    )(hidden, own, other, held)


def second_near(even, odd, rights):
    planes, rows, _ = even.shape
    return pl.pallas_call(
        second_near_kernel,
        out_shape=jax.ShapeDtypeStruct(
            (2, (planes - 2) * rows // 4, rights.shape[2]), jnp.bfloat16
        ),
        in_specs=[pl.BlockSpec(memory_space=pltpu.VMEM)] * 3,
        out_specs=pl.BlockSpec(memory_space=pltpu.VMEM),
        compiler_params=pltpu.CompilerParams(vmem_limit_bytes=32 * 2**20),
    )(even, odd, rights)


def stationary(
    coarse, skip, up_weight, up_bias, first_weight, first_bias, second_weight, second_bias
):
    s, d, c = (lax.axis_index(a) for a in ("space", "dp", "chan"))
    group = ("space", "dp", "chan")
    _, _, cx, cy, cin = coarse.shape
    _, bx, fy, fz, half = skip.shape
    fx = 4 * bx
    cells = cx * cy
    block = bx * fy * fz
    taps, kb, _, own_n = up_weight.shape
    up_rows = taps * own_n
    first_own = first_weight[:, :, 0, :].transpose(0, 2, 1)
    up_rows_own = up_weight[:, :, 0, :].transpose(0, 2, 1).reshape(up_rows, kb)
    columns = coarse.reshape(cells, cin)
    columns = [columns[:, i : i + kb] for i in range(0, cin, kb)]
    up_packet = jnp.concatenate([up_rows_own] + columns, axis=0)
    skip_rows = skip.reshape(block, half)
    skip_packet = jnp.pad(skip_rows, ((0, up_packet.shape[0] - block), (0, 0)))
    early = jnp.where(s < 2, up_packet, skip_packet)
    late = jnp.where(s < 2, skip_packet, up_packet)
    span = (first_own.shape[0] + 1) // 2
    start = lax.axis_index("groups") * (first_own.shape[0] - span)
    near = lax.dynamic_slice_in_dim(first_own, start, span, 0)
    held = jnp.stack([up_bias, first_bias, second_bias])
    early_route, late_route, cross_route = line_routes()
    late = lax.ppermute(late, group, late_route)
    late_other = swapped(late[:up_rows], "dp")
    early = lax.ppermute(early, group, early_route)
    early_other = lax.ppermute(up_rows_own, group, cross_route)
    near = swapped(near, "dp")
    far = swapped(near, "groups")
    second_raw, late = lax.optimization_barrier((second_weight[:, :, 0, :], late))
    second_own = dense(second_raw)
    second_own, late_other = lax.optimization_barrier((second_own, late_other))
    second_other = swapped(second_own, "dp")
    slabs = swapped(jnp.stack([early[up_rows:], late[up_rows:]]), "chan")
    part = up_part(early, late, early_other, late_other, slabs, held, fx * fy * fz)
    part_other = swapped(part, "chan")
    first_other = other_weights(near, far, first_own.shape[0])
    first, tile = first_conv(part, part_other, first_own, first_other, fx)
    mine, theirs = (pick(first, c), swapped(pick(first, 1 - c), "chan"))
    chunks = jnp.stack([mine, theirs]).reshape(4, block, half)

    def chunk_for(plane):
        return pick(chunks, 2 * ((plane // 2) ^ c) + ((plane % 2) ^ d))

    terms = terms_of([(step, chunk_for(s ^ step)) for step in (3, 2, 1)])
    terms[0], second_other = lax.optimization_barrier((terms[0], second_other))
    total = summed(chunk_for(s).astype(jnp.float32) + tile[:1], terms)
    hidden = jax.nn.silu(total).astype(jnp.bfloat16)
    hidden = ordered(c, hidden, swapped(hidden, "chan"), 0)
    away, tile, even, odd, rights = second_far(hidden, second_own, second_other, held, fx)
    sends = [(3, pick(away, (s + 1) % 2)), (2, pick(away, s % 2))]
    terms = terms_of(sends)
    even, sends = lax.optimization_barrier((even, sends))
    home = second_near(even, odd, rights)
    terms += terms_of([(1, pick(home, (s + 1) % 2))])
    total = summed(pick(home, s % 2).astype(jnp.float32) + tile[:1], terms)
    return total.astype(jnp.bfloat16).reshape(skip.shape)


def keeps_weights(mesh):
    sizes = tuple(mesh.shape[a] for a in ("groups", "space", "dp", "chan"))
    return sizes == (2, 4, 2, 2)


def solution(mesh):
    return jax.shard_map(
        stationary if keeps_weights(mesh) else body,
        mesh=mesh,
        in_specs=(
            P(("groups", "dp"), "space", None, None, None),
            P(("groups", "dp"), "space", None, None, "chan"),
            P(None, "space", "chan", "dp"),
            P("chan"),
            P(None, "space", "chan", "dp"),
            P("chan"),
            P(None, "space", "chan", "dp"),
            P("chan"),
        ),
        out_specs=P(("groups", "dp"), "space", None, None, "chan"),
        check_vma=False,
    )
```

```python
import jax
import jax.numpy as jnp
from jax import lax
from jax.experimental import pallas as pl
from jax.experimental.pallas import tpu as pltpu
from jax.sharding import PartitionSpec as P


def padded_2(array, sides, width):
    for axis, dim in sides:
        peers, length = (lax.axis_size(axis), array.shape[dim])
        up = [(i, (i + 1) % peers) for i in range(peers - 1)]
        down = [(j, i) for i, j in up]
        last = lax.slice_in_dim(array, length - width, length, axis=dim)
        first = lax.slice_in_dim(array, 0, width, axis=dim)
        before = lax.ppermute(last, axis, up)
        after = lax.ppermute(first, axis, down)
        array = jnp.concatenate([before, array, after], axis=dim)
    return array


def alternate(total, bias):
    samples, depth_cells, width_cells, height_cells, taps, outputs = total.shape
    grid = total.reshape(samples, depth_cells, width_cells, height_cells, 2, 2, 2, outputs)
    grid = grid.transpose(0, 2, 4, 3, 5, 1, 6, 7)
    grid = grid.reshape(samples, 2 * width_cells, 2 * height_cells, 2 * depth_cells, outputs)
    return (grid + bias).astype(jnp.bfloat16)


def upsample_block(coarse, up_weight):
    columns = lax.all_gather(up_weight, "dp", axis=3, tiled=True)[:, :, 0, :]
    initial = jnp.zeros(coarse.shape[:4] + (8, columns.shape[2]), jnp.float32)

    def accumulate(summed, weight_rows, offset):
        return jnp.einsum(
            "szxyi,kio->szxyko", coarse, weight_rows, preferred_element_type=jnp.float32
        )

    return accumulate(initial, lax.all_gather(columns, "space", axis=1, tiled=True), jnp.int32(0))


def spatial_conv(padded, weight_block):
    kernel = weight_block.reshape(3, 3, 3, weight_block.shape[1], weight_block.shape[2])
    return lax.conv_general_dilated(
        padded,
        kernel,
        (1, 1, 1),
        [(0, 0), (1, 1), (1, 1)],
        dimension_numbers=("NDHWC", "DHWIO", "NDHWC"),
        preferred_element_type=jnp.float32,
    )


def folded_conv(padded, columns, base_shape):
    initial = jnp.zeros(base_shape + (columns.shape[2],), jnp.float32)

    def accumulate(summed, weight_rows, offset):
        sliced = lax.dynamic_slice_in_dim(padded, offset, weight_rows.shape[1], 4)
        return summed + spatial_conv(sliced, weight_rows)

    return (accumulate, initial)


def body(coarse, skip, up_weight, up_bias, first_weight, first_bias, second_weight, second_bias):
    slabs = lax.all_to_all(coarse, "space", split_axis=2, concat_axis=1, tiled=True)
    upsampled = alternate(upsample_block(slabs, up_weight), up_bias)
    up_full, skip_full = (
        lax.all_gather(upsampled, "chan", axis=4, tiled=True),
        lax.all_gather(skip, "chan", axis=4, tiled=True),
    )
    joined = jnp.concatenate([up_full, skip_full], axis=4)
    padded = padded_2(joined, (("space", 1),), 1)
    base_shape = joined.shape[:4]
    first_columns = lax.all_gather(first_weight, "dp", axis=3, tiled=True)[:, :, 0, :]
    accumulate, initial = folded_conv(padded, first_columns, base_shape)
    first = accumulate(
        initial, lax.all_gather(first_columns, "space", axis=1, tiled=True), jnp.int32(0)
    )
    hidden = jax.nn.silu(first + first_bias).astype(jnp.bfloat16)
    hidden_full = lax.all_gather(hidden, "chan", axis=4, tiled=True)
    hidden_padded = padded_2(hidden_full, (("space", 1),), 1)
    second_columns = lax.all_gather(second_weight, "dp", axis=3, tiled=True)[:, :, 0, :]
    accumulate_two, initial_two = folded_conv(hidden_padded, second_columns, base_shape)
    second = accumulate_two(
        initial_two, lax.all_gather(second_columns, "space", axis=1, tiled=True), jnp.int32(0)
    )
    return (second + second_bias).astype(jnp.bfloat16)


def swapped(array, axis):
    return lax.ppermute(array, axis, [(0, 1), (1, 0)])


def ordered(index, own, other, axis=0):
    first = jnp.where(index == 0, own, other)
    second = jnp.where(index == 0, other, own)
    return jnp.stack([first, second], axis=axis)


def dense_kernel(weight, out):
    deep = weight.shape[1] // 2
    for tap in range(weight.shape[0]):
        out[tap] = jnp.concatenate([weight[tap, :deep], weight[tap, deep:]], axis=1)


def dense(weight):
    taps, rows, lanes = weight.shape
    return pl.pallas_call(
        dense_kernel,
        out_shape=jax.ShapeDtypeStruct((taps, rows // 2, 2 * lanes), weight.dtype),
        in_specs=[pl.BlockSpec(memory_space=pltpu.VMEM)],
        out_specs=pl.BlockSpec(memory_space=pltpu.VMEM),
        compiler_params=pltpu.CompilerParams(vmem_limit_bytes=16 * 2**20),
    )(weight)


def up_kernel(early, late, early_other, late_other, slabs, held, part):
    s, d, c = (lax.axis_index(a) for a in ("space", "dp", "chan"))
    rows, kb = early_other.shape
    deep = slabs.shape[1] // 4
    taps = 8
    own_n = rows // taps
    half = part.shape[1]
    all_cells = part.shape[0] - 8
    block = all_cells // 4
    part[pl.ds(all_cells, 8)] = jnp.broadcast_to(held[1:2], (8, half))

    @pl.when(s < 2)
    def _():
        lefts, rights = ([], [])
        for k in range(2):
            pieces = []
            for parity in range(2):
                for i, packet in enumerate((early, late)):
                    low = packet[pl.ds(rows + 2 * k * deep, deep)]
                    high = packet[pl.ds(rows + (2 * k + 1) * deep, deep)]
                    mine = jnp.where(c == 0, low, high)
                    low = slabs[i, pl.ds(2 * k * deep, deep)]
                    high = slabs[i, pl.ds((2 * k + 1) * deep, deep)]
                    theirs = jnp.where(c == 0, low, high)
                    pieces.append(jnp.where(c == parity, mine, theirs))
            lefts.append(jnp.concatenate(pieces, axis=0))
            packet, other = ((early, early_other), (late, late_other))[k]
            pieces = []
            for tap in range(taps):
                one = packet[pl.ds(tap * own_n, own_n)]
                two = other[pl.ds(tap * own_n, own_n)]
                pieces += [jnp.where(d == 0, one, two), jnp.where(d == 0, two, one)]
            rights.append(jnp.concatenate(pieces, axis=0))
        left = jnp.concatenate(lefts, axis=1)
        right = jnp.concatenate(rights, axis=1)
        bias = held[0:1] * jnp.where(c == s, 1.0, 0.0)
        for tap in range(taps):
            a, b, cc = (tap // 4, tap // 2 % 2, tap % 2)
            total = lax.dot_general(
                left,
                right[tap * 2 * own_n : (tap + 1) * 2 * own_n],
                NT,
                preferred_element_type=jnp.float32,
            )
            total = total + bias
            for parity in range(2):
                for i in range(2):
                    z = 2 * (parity + 2 * i) + cc
                    for x in range(deep // 8):
                        at = (parity * 2 + i) * deep + x * 8
                        start = ((2 * x + a) * 16 + b) * 8 + z
                        part[pl.ds(start, 8, 16)] = total[at : at + 8]

    @pl.when(s >= 2)
    def _():
        for i, packet in enumerate((late, early)):
            values = packet[pl.ds(0, block)].astype(jnp.float32)
            for parity in range(2):
                place = pl.ds((2 * i + parity) * block, block)
                part[place] = jnp.where(c == parity, values, 0.0)


def up_part(early, late, early_other, late_other, slabs, held, cells):
    return pl.pallas_call(
        up_kernel,
        out_shape=jax.ShapeDtypeStruct((cells + 8, held.shape[1]), jnp.float32),
        in_specs=[pl.BlockSpec(memory_space=pltpu.VMEM)] * 6,
        out_specs=pl.BlockSpec(memory_space=pltpu.VMEM),
        compiler_params=pltpu.CompilerParams(vmem_limit_bytes=32 * 2**20),
        cost_estimate=pl.CostEstimate(flops=1000, bytes_accessed=1000, transcendentals=0),
    )(early, late, early_other, late_other, slabs, held)


def terms_of(chunks):
    terms = []
    for step, chunk in chunks:
        terms.append(lax.ppermute(chunk, "space", [(i, i ^ step) for i in range(4)]))
    return terms


def summed(start, terms):
    for term in terms:
        start = start + term.astype(jnp.float32)
    return start


def pick(pair, index):
    return lax.dynamic_index_in_dim(pair, index, 0, keepdims=False)


def line_routes():
    early, late, cross = ([], [], [])
    for s in range(4):
        for d in range(2):
            for c in range(2):
                source = (s * 2 + d) * 2 + c
                up_target = (c * 2 + d) * 2 + s % 2
                skip_target = ((2 + c) * 2 + d) * 2 + s % 2
                early.append((source, up_target if s < 2 else skip_target))
                late.append((source, skip_target if s < 2 else up_target))
                if s < 2:
                    cross.append((source, (c * 2 + 1 - d) * 2 + s % 2))
    return early, late, cross


NT = (((1,), (1,)), ((), ()))
NN = (((1,), (0,)), ((), ()))


def build_taps(planes_of, even, odd):
    planes = even.shape[0] - 2
    rows, width = even.shape[1:]
    blank = jnp.zeros((1,) + odd.shape[1:], odd.dtype)
    odd[0:1] = blank
    odd[planes + 1 : planes + 2] = blank
    even[0:1] = blank[:, :rows]
    even[planes + 1 : planes + 2] = blank[:, :rows]
    edge = jnp.zeros((8, width), jnp.float32)
    for x, taps in planes_of():
        even[x + 1] = taps.astype(jnp.bfloat16)
        odd[x + 1] = jnp.concatenate([edge, taps, edge], axis=0).astype(jnp.bfloat16)


def half_product(q, even, odd, right_of, form):
    planes = even.shape[0] - 2
    rows = even.shape[1]
    total = None
    for dx in range(3):
        for dy in range(3):
            at = pl.ds(q * (planes // 2) + dx, planes // 2)
            left = even[at] if dy == 1 else odd[at, pl.ds(8 * dy, rows)]
            right = right_of(dx * 3 + dy)
            width = right.shape[1] if form is NT else right.shape[0]
            left = left.reshape(planes // 2 * rows, left.shape[2])[:, :width]
            term = lax.dot_general(left, right, form, preferred_element_type=jnp.float32)
            total = term if total is None else total + term
    return total


def other_kernel(near, far, out):
    g = lax.axis_index("groups")
    span, taps = (near.shape[0], out.shape[0])
    for tap in range(taps):
        if tap < span:
            lower, upper = (near[tap], far[tap])
        else:
            lower, upper = (far[tap - taps + span], near[tap - taps + span])
        if tap == span - 1:
            upper = near[0]
        out[tap] = jnp.where(g == 0, lower, upper)


def other_weights(near, far, taps):
    return pl.pallas_call(
        other_kernel,
        out_shape=jax.ShapeDtypeStruct((taps,) + near.shape[1:], near.dtype),
        in_specs=[pl.BlockSpec(memory_space=pltpu.VMEM)] * 2,
        out_specs=pl.BlockSpec(memory_space=pltpu.VMEM),
        compiler_params=pltpu.CompilerParams(vmem_limit_bytes=16 * 2**20),
        cost_estimate=pl.CostEstimate(flops=10000000000, bytes_accessed=0, transcendentals=0),
    )(near, far)


def first_right(own, other):
    def right_of(group):
        pairs = [jnp.concatenate([own[i], other[i]], axis=0) for i in range(3 * group, 3 * group + 3)]
        return jnp.concatenate(pairs, axis=1)

    return right_of


def first_out(total, out, q):
    half = total.shape[1]
    swap = half // 2
    low, high = (total[: total.shape[0] // 2], total[total.shape[0] // 2 :])
    lane = lax.broadcasted_iota(jnp.int32, low.shape, 1)
    out[q, 0] = jnp.where(lane < swap, low, pltpu.roll(high, swap, 1)).astype(jnp.bfloat16)
    out[q, 1] = jnp.where(lane < swap, pltpu.roll(low, swap, 1), high).astype(jnp.bfloat16)


def first_kernel(mine, theirs, own, other, out, tile, even, odd):
    s, c = (lax.axis_index(a) for a in ("space", "chan"))
    rows = even.shape[1]
    half = mine.shape[1]
    cells = mine.shape[0] - 8
    cell = lax.broadcasted_iota(jnp.int32, (rows, half), 0) % 8

    def planes_of():
        for x in range(cells // rows):
            plane = mine[x * rows : (x + 1) * rows] + theirs[x * rows : (x + 1) * rows]
            plane = plane.astype(jnp.bfloat16).astype(jnp.float32)
            below = jnp.where(cell == 0, 0.0, pltpu.roll(plane, 1, 0))
            above = jnp.where(cell == 7, 0.0, pltpu.roll(plane, rows - 1, 0))
            yield x, jnp.concatenate([below, plane, above], axis=1)

    build_taps(planes_of, even, odd)
    right_of = first_right(own, other)
    for q in range(2):
        first_out(half_product(q, even, odd, right_of, NT), out, q)
    bias = jnp.where(s // 2 == c, mine[pl.ds(cells, 8)], theirs[pl.ds(cells, 8)])
    turned = pltpu.roll(bias, half // 2, 1)
    lane = lax.broadcasted_iota(jnp.int32, bias.shape, 1)
    tile[...] = jnp.where((lane < half // 2) == (s % 2 == 0), bias, turned)


def first_conv(mine, theirs, own, other, planes):
    cells, half = (mine.shape[0] - 8, mine.shape[1])
    rows = cells // planes
    return pl.pallas_call(
        first_kernel,
        out_shape=(
            jax.ShapeDtypeStruct((2, 2, cells // 4, half), jnp.bfloat16),
            jax.ShapeDtypeStruct((8, half), jnp.float32),
        ),
        in_specs=[pl.BlockSpec(memory_space=pltpu.VMEM)] * 4,
        out_specs=[pl.BlockSpec(memory_space=pltpu.VMEM)] * 2,
        scratch_shapes=[
            pltpu.VMEM((planes + 2, rows, 3 * half), jnp.bfloat16),
            pltpu.VMEM((planes + 2, rows + 16, 3 * half), jnp.bfloat16),
        ],
        compiler_params=pltpu.CompilerParams(vmem_limit_bytes=32 * 2**20),
    )(mine, theirs, own, other)


def second_far_kernel(hidden, own, other, held, out, tile, even, odd, rights):
    s, d = (lax.axis_index(a) for a in ("space", "dp"))
    rows = even.shape[1]
    lanes = hidden.shape[2]
    swap = lanes // 2
    cell = lax.broadcasted_iota(jnp.int32, (rows, lanes), 0) % 8
    low = lax.broadcasted_iota(jnp.int32, (rows, lanes), 1) < swap
    per = hidden.shape[1] // rows

    def planes_of():
        for q in range(2):
            for r in range(per):
                packed = hidden[q, r * rows : (r + 1) * rows].astype(jnp.float32)
                turned = pltpu.roll(packed, swap, 1)
                for u in range(2):
                    here, there = (packed, turned) if u == 0 else (turned, packed)
                    below = jnp.where(cell == 0, 0.0, pltpu.roll(here, 1, 0))
                    above = jnp.where(cell == 7, 0.0, pltpu.roll(here, rows - 1, 0))
                    taps = [jnp.where(low, below, there), jnp.where(low, above, 0.0)]
                    yield (q * 2 + u) * per + r, jnp.concatenate(taps, axis=1)

    build_taps(planes_of, even, odd)
    low = lax.broadcasted_iota(jnp.int32, own.shape[1:], 1) < swap
    for group in range(own.shape[0] // 3):
        pieces = []
        for tap in range(3 * group, 3 * group + 3):
            one = jnp.where(d == 0, own[tap], other[tap])
            two = jnp.where(d == 0, other[tap], own[tap])
            pieces.append(jnp.where(low, one, pltpu.roll(two, swap, 1)))
            pieces.append(jnp.where(low, pltpu.roll(one, swap, 1), two))
        rights[group] = jnp.concatenate(pieces, axis=0)
    total = half_product(1 - s // 2, even, odd, lambda group: rights[group], NN)
    out[...] = total.astype(jnp.bfloat16).reshape(out.shape)
    tile[...] = jnp.broadcast_to(held[2:3], tile.shape)


def second_near_kernel(even, odd, rights, out):
    s = lax.axis_index("space")
    total = half_product(s // 2, even, odd, lambda group: rights[group], NN)
    out[...] = total.astype(jnp.bfloat16).reshape(out.shape)


def second_far(hidden, own, other, held, planes):
    _, rows2, lanes = hidden.shape
    rows = rows2 * 4 // planes
    return pl.pallas_call(
        second_far_kernel,
        out_shape=(
            jax.ShapeDtypeStruct((2, rows2, lanes), jnp.bfloat16),
            jax.ShapeDtypeStruct((8, lanes), jnp.float32),
            jax.ShapeDtypeStruct((planes + 2, rows, 2 * lanes), jnp.bfloat16),
            jax.ShapeDtypeStruct((planes + 2, rows + 16, 2 * lanes), jnp.bfloat16),
            jax.ShapeDtypeStruct((9, 6 * own.shape[1], lanes), jnp.bfloat16),
        ),
        in_specs=[pl.BlockSpec(memory_space=pltpu.VMEM)] * 4,
        out_specs=[pl.BlockSpec(memory_space=pltpu.VMEM)] * 5,
        compiler_params=pltpu.CompilerParams(vmem_limit_bytes=32 * 2**20),
    )(hidden, own, other, held)


def second_near(even, odd, rights):
    planes, rows, _ = even.shape
    return pl.pallas_call(
        second_near_kernel,
        out_shape=jax.ShapeDtypeStruct(
            (2, (planes - 2) * rows // 4, rights.shape[2]), jnp.bfloat16
        ),
        in_specs=[pl.BlockSpec(memory_space=pltpu.VMEM)] * 3,
        out_specs=pl.BlockSpec(memory_space=pltpu.VMEM),
        compiler_params=pltpu.CompilerParams(vmem_limit_bytes=32 * 2**20),
    )(even, odd, rights)


def stationary(
    coarse, skip, up_weight, up_bias, first_weight, first_bias, second_weight, second_bias
):
    s, d, c = (lax.axis_index(a) for a in ("space", "dp", "chan"))
    group = ("space", "dp", "chan")
    _, _, cx, cy, cin = coarse.shape
    _, bx, fy, fz, half = skip.shape
    fx = 4 * bx
    cells = cx * cy
    block = bx * fy * fz
    taps, kb, _, own_n = up_weight.shape
    up_rows = taps * own_n
    first_own = first_weight[:, :, 0, :].transpose(0, 2, 1)
    up_rows_own = up_weight[:, :, 0, :].transpose(0, 2, 1).reshape(up_rows, kb)
    columns = coarse.reshape(cells, cin)
    columns = [columns[:, i : i + kb] for i in range(0, cin, kb)]
    up_packet = jnp.concatenate([up_rows_own] + columns, axis=0)
    skip_rows = skip.reshape(block, half)
    skip_packet = jnp.pad(skip_rows, ((0, up_packet.shape[0] - block), (0, 0)))
    early = jnp.where(s < 2, up_packet, skip_packet)
    late = jnp.where(s < 2, skip_packet, up_packet)
    span = (first_own.shape[0] + 1) // 2
    start = lax.axis_index("groups") * (first_own.shape[0] - span)
    near = lax.dynamic_slice_in_dim(first_own, start, span, 0)
    held = jnp.stack([up_bias, first_bias, second_bias])
    early_route, late_route, cross_route = line_routes()
    late = lax.ppermute(late, group, late_route)
    late_other = swapped(late[:up_rows], "dp")
    early = lax.ppermute(early, group, early_route)
    early_other = lax.ppermute(up_rows_own, group, cross_route)
    near = swapped(near, "dp")
    far = swapped(near, "groups")
    second_raw, late = lax.optimization_barrier((second_weight[:, :, 0, :], late))
    second_own = dense(second_raw)
    second_own, late_other = lax.optimization_barrier((second_own, late_other))
    second_other = swapped(second_own, "dp")
    slabs = swapped(jnp.stack([early[up_rows:], late[up_rows:]]), "chan")
    part = up_part(early, late, early_other, late_other, slabs, held, fx * fy * fz)
    part_other = swapped(part, "chan")
    first_other = other_weights(near, far, first_own.shape[0])
    first, tile = first_conv(part, part_other, first_own, first_other, fx)
    mine, theirs = (pick(first, c), swapped(pick(first, 1 - c), "chan"))
    theirs, second_other = lax.optimization_barrier((theirs, second_other))
    chunks = jnp.stack([mine, theirs]).reshape(4, block, half)

    def chunk_for(plane):
        return pick(chunks, 2 * ((plane // 2) ^ c) + ((plane % 2) ^ d))

    terms = terms_of([(step, chunk_for(s ^ step)) for step in (3, 2, 1)])
    total = summed(chunk_for(s).astype(jnp.float32) + tile[:1], terms)
    hidden = jax.nn.silu(total).astype(jnp.bfloat16)
    hidden = ordered(c, hidden, swapped(hidden, "chan"), 0)
    away, tile, even, odd, rights = second_far(hidden, second_own, second_other, held, fx)
    sends = [(3, pick(away, (s + 1) % 2)), (2, pick(away, s % 2))]
    terms = terms_of(sends)
    even, sends = lax.optimization_barrier((even, sends))
    home = second_near(even, odd, rights)
    terms += terms_of([(1, pick(home, (s + 1) % 2))])
    total = summed(pick(home, s % 2).astype(jnp.float32) + tile[:1], terms)
    return total.astype(jnp.bfloat16).reshape(skip.shape)


def keeps_weights(mesh):
    sizes = tuple(mesh.shape[a] for a in ("groups", "space", "dp", "chan"))
    return sizes == (2, 4, 2, 2)


def solution(mesh):
    return jax.shard_map(
        stationary if keeps_weights(mesh) else body,
        mesh=mesh,
        in_specs=(
            P(("groups", "dp"), "space", None, None, None),
            P(("groups", "dp"), "space", None, None, "chan"),
            P(None, "space", "chan", "dp"),
            P("chan"),
            P(None, "space", "chan", "dp"),
            P("chan"),
            P(None, "space", "chan", "dp"),
            P("chan"),
        ),
        out_specs=P(("groups", "dp"), "space", None, None, "chan"),
        check_vma=False,
    )
```
